32 devices in a mesh: groups: 2 (over y), member: 4 (over z), fsdp: 4 (over x, core).
Axes of the slice: x: 2, y: 2, z: 4, core: 2. Of those that a mesh axis runs over, the one named last changes fastest.
Arguments:
- tokens: bfloat16 [8, 768, 4096], P(('groups', 'member'), 'fsdp'), parts along dimension 0, may hold values from -6 to 6
- grad_out: bfloat16 [8, 768, 4096], P(('groups', 'member'), 'fsdp'), parts along dimension 0, may hold values from -6 to 6
- gate_up: bfloat16 [8, 4096, 256], P(('groups', 'member'), 'fsdp'), parts along dimension 0, may hold values from -6 to 6
- down: bfloat16 [8, 128, 4096], P(('groups', 'member'), 'fsdp'), parts along dimension 0, may hold values from -6 to 6
- mom1_gate_up: float32 [8, 4096, 256], P(('groups', 'member'), 'fsdp'), parts along dimension 0, may hold values from -4 to 4
- mom2_gate_up: float32 [8, 4096, 256], P(('groups', 'member'), 'fsdp'), parts along dimension 0, may hold values from 0.1 to 4
- mom1_down: float32 [8, 128, 4096], P(('groups', 'member'), 'fsdp'), parts along dimension 0, may hold values from -4 to 4
- mom2_down: float32 [8, 128, 4096], P(('groups', 'member'), 'fsdp'), parts along dimension 0, may hold values from 0.1 to 4
- learning: float32 [8], P('groups'), parts along dimension 0, may hold values from 0.02 to 0.2
- winner: int32 [8], P('groups'), parts along dimension 0, may hold values from 0 to 3, as said below
Outputs:
- new_gate_up: bfloat16 [8, 4096, 256], P(('groups', 'member'), 'fsdp'), parts along dimension 0
- new_down: bfloat16 [8, 128, 4096], P(('groups', 'member'), 'fsdp'), parts along dimension 0
- new_mom1_gate_up: float32 [8, 4096, 256], P(('groups', 'member'), 'fsdp'), parts along dimension 0
- new_mom2_gate_up: float32 [8, 4096, 256], P(('groups', 'member'), 'fsdp'), parts along dimension 0
- new_mom1_down: float32 [8, 128, 4096], P(('groups', 'member'), 'fsdp'), parts along dimension 0
- new_mom2_down: float32 [8, 128, 4096], P(('groups', 'member'), 'fsdp'), parts along dimension 0
The draws below stay inside these ranges and needn't reach their ends.
There are 2 independent parts, one for each index of `groups`. The reference program is written for one: setup_inputs(seed, part) draws one part's arguments, and reference() takes and returns one part's arrays. A program takes and returns all parts, laid end to end along the dimension named above; each array names one. Nothing has to cross between parts.
Inputs may be any that keep to these rules, and one draw needn't show every extreme that they name: Every winner names itself; a member that names another member is named by no one; no member is named by more than four others, and some member is named by four others (by half of the members where there are fewer than eight).
All inputs are finite; a program needn't handle non-finite values.
Results may differ from the reference program's by a relative error of at most 0.008.
Values may be sent and summed in bfloat16 or wider, within the bound.
No kernel may reach another device: no remote copies, remote signals or barrier semaphores. Data moves between devices by JAX's collectives and lax.ppermute only.
A program may use at most 64 MiB of HBM per device.

```python
import math
import jax
import jax.numpy as jnp
from jax import lax

D = 4096
UNITS = 128
TOK_DEV = 192
MEMBERS = 4
TOKENS = 768
N_FSDP = 4


def draw_winner(key, part):
    key = jax.random.fold_in(key, 7)
    shuffled = jax.random.permutation(key, MEMBERS)
    num_winners = max(1, MEMBERS // 4)
    num_losers = MEMBERS // 2
    slots = jnp.arange(num_losers)
    picks = jnp.where(slots < 4, 0, 1 + (slots - 4) % max(num_winners - 1, 1))
    result = jnp.arange(MEMBERS).astype(jnp.int32)
    result = result.at[shuffled[num_winners:num_winners + num_losers]].set(shuffled[picks])
    return result.astype(jnp.int32)


def shard_levels(key, shape, shards, low, high):
    def one(position, shards_of):
        steps = jax.random.uniform(jax.random.fold_in(jax.random.fold_in(key, 6), position), (shards_of,), jnp.float32, low / len(shards), high / len(shards))
        return jnp.repeat(jnp.exp(steps), shape[position] // shards_of).reshape((-1,) + (1,) * (len(shape) - position - 1))

    factor_of = one(*shards[0])
    for cut in shards[1:]:
        factor_of = factor_of * one(*cut)
    return factor_of


def scatter_about(own_key, dims, scale, limit, cuts=(), kind=jnp.bfloat16):
    values = scale * jax.random.normal(own_key, dims, jnp.float32)
    if cuts:
        values = values * shard_levels(own_key, dims, cuts, -0.22, 0.18)
    return jnp.clip(values, -limit, limit).astype(kind)


def setup_inputs(seed: int = 0, part: int = 0) -> dict:
    keys = jax.random.split(jax.random.key(seed), 11)
    part_splits = jax.random.split(jax.random.fold_in(keys[10], part), 11)
    tokens = scatter_about(part_splits[0], (MEMBERS, TOKENS, D), 1.0, 6.0, ((0, 4), (1, 4)))
    grad_out = scatter_about(part_splits[1], (MEMBERS, TOKENS, D), 1.0, 6.0, ((0, 4), (1, 4)))
    gate_up = scatter_about(part_splits[2], (MEMBERS, D, 2 * UNITS), 1.0, 6.0, ((0, 4), (1, 4)))
    down = scatter_about(part_splits[3], (MEMBERS, UNITS, D), 1.0, 6.0, ((0, 4), (1, 4)))
    mom1_gate_up = scatter_about(part_splits[4], (MEMBERS, D, 2 * UNITS), 0.5, 4.0, ((0, 4), (1, 4)), jnp.float32)
    mom2_gate_up = jnp.clip(jnp.exp(math.log(4.0) - 3.6888794 * jax.random.uniform(part_splits[5], (MEMBERS, D, 2 * UNITS), jnp.float32) ** shard_levels(part_splits[5], (MEMBERS, D, 2 * UNITS), ((0, 4), (1, 4)), -0.2, 0.2)), 0.1, 4.0)
    mom1_down = scatter_about(part_splits[6], (MEMBERS, UNITS, D), 0.5, 4.0, ((0, 4), (1, 4)), jnp.float32)
    mom2_down = jnp.clip(jnp.exp(math.log(4.0) - 3.6888794 * jax.random.uniform(part_splits[7], (MEMBERS, UNITS, D), jnp.float32) ** shard_levels(part_splits[7], (MEMBERS, UNITS, D), ((0, 4), (1, 4)), -0.2, 0.2)), 0.1, 4.0)
    learning = jnp.clip(jnp.exp(jax.random.uniform(part_splits[8], (MEMBERS,), jnp.float32, math.log(0.02), math.log(0.2))), 0.02, 0.2)
    winner = draw_winner(jax.random.fold_in(jax.random.fold_in(keys[10], part), 71), part)
    return dict(tokens=tokens, grad_out=grad_out, gate_up=gate_up, down=down, mom1_gate_up=mom1_gate_up, mom2_gate_up=mom2_gate_up, mom1_down=mom1_down, mom2_down=mom2_down, learning=learning, winner=winner)


beta_one = 0.9
beta_two = 0.95
epsilon = 1e-08
decay = 0.1

def adamw(weight, grad, first, second, rate):
    first_new = beta_one * first + (1.0 - beta_one) * grad
    second_new = beta_two * second + (1.0 - beta_two) * grad * grad
    wide = weight.astype(jnp.float32)
    updated = wide - rate * (first_new / (jnp.sqrt(second_new) + epsilon) + decay * wide)
    return (updated.astype(jnp.bfloat16), first_new, second_new)

def member_step(inputs):
    rows_in, upstream, w_gate_up, w_down, first_gu, second_gu, first_dn, second_dn, rate = inputs
    preact = jnp.dot(rows_in, w_gate_up, preferred_element_type=jnp.float32) * D ** (-0.5)
    gate = preact[:, :UNITS]
    upper = preact[:, UNITS:]
    sigma = jax.nn.sigmoid(gate)
    active = gate * sigma
    hidden = (active * upper).astype(jnp.bfloat16)
    dhidden = jnp.dot(upstream, w_down.T, preferred_element_type=jnp.float32) * UNITS ** (-0.5)
    dgate = dhidden * upper * (sigma * (1.0 + gate * (1.0 - sigma)))
    dupper = dhidden * active
    dpreact = (jnp.concatenate([dgate, dupper], axis=1) * D ** (-0.5)).astype(jnp.bfloat16)
    blocks_in = rows_in.reshape(N_FSDP, TOK_DEV, D).astype(jnp.float32)
    blocks_dp = dpreact.reshape(N_FSDP, TOK_DEV, 2 * UNITS).astype(jnp.float32)
    partial_gu = jnp.einsum('btd,btk->bdk', blocks_in, blocks_dp).astype(jnp.bfloat16)
    partial_gu = lax.optimization_barrier(partial_gu)
    grad_gu = lax.optimization_barrier(jnp.sum(partial_gu.astype(jnp.float32), axis=0))
    blocks_hid = hidden.reshape(N_FSDP, TOK_DEV, UNITS).astype(jnp.float32)
    blocks_up = upstream.reshape(N_FSDP, TOK_DEV, D).astype(jnp.float32)
    partial_dn = (jnp.einsum('bth,btd->bhd', blocks_hid, blocks_up) * UNITS ** (-0.5)).astype(jnp.bfloat16)
    partial_dn = lax.optimization_barrier(partial_dn)
    grad_dn = lax.optimization_barrier(jnp.sum(partial_dn.astype(jnp.float32), axis=0))
    new_gu, new_first_gu, new_second_gu = adamw(w_gate_up, grad_gu, first_gu, second_gu, rate)
    new_dn, new_first_dn, new_second_dn = adamw(w_down, grad_dn, first_dn, second_dn, rate)
    return (new_gu, new_dn, new_first_gu, new_second_gu, new_first_dn, new_second_dn)

def reference(tokens, grad_out, gate_up, down, mom1_gate_up, mom2_gate_up, mom1_down, mom2_down, learning, winner):
    source = winner.astype(jnp.int32)
    inputs = (tokens, grad_out, jnp.take(gate_up, source, axis=0), jnp.take(down, source, axis=0), jnp.take(mom1_gate_up, source, axis=0), jnp.take(mom2_gate_up, source, axis=0), jnp.take(mom1_down, source, axis=0), jnp.take(mom2_down, source, axis=0), jnp.take(learning, source, axis=0))
    results = lax.map(member_step, inputs)
    return (results[0], results[1], results[2], results[3], results[4], results[5])
```

```python
import jax
import jax.numpy as jnp
from jax import lax
from jax.sharding import PartitionSpec as P

beta_one = 0.9
beta_two = 0.95
epsilon = 1e-08
decay = 0.1


def spread(block, axis, source):
    block = jnp.where(lax.axis_index(axis) == source, block, jnp.zeros_like(block))
    return lax.psum(block, axis)


def adamw(weight, grad, first, second, rate):
    first_new = beta_one * first + (1.0 - beta_one) * grad
    second_new = beta_two * second + (1.0 - beta_two) * grad * grad
    wide = weight.astype(jnp.float32)
    updated = wide - rate * (first_new / (jnp.sqrt(second_new) + epsilon) + decay * wide)
    return (updated.astype(jnp.bfloat16), first_new, second_new)


def on_device_any(
    tokens,
    grad_out,
    gate_up,
    down,
    mom1_gate_up,
    mom2_gate_up,
    mom1_down,
    mom2_down,
    learning,
    winner,
):
    members = lax.axis_size("member")
    member_index = lax.axis_index("member")
    rows_in = tokens[0]
    upstream = grad_out[0]
    width = rows_in.shape[1]
    units = gate_up.shape[2] // 2
    shard_gu = gate_up[0]
    shard_dn = down[0]
    cut = shard_gu.size // members

    def joined(first_part, second_part):
        return jnp.concatenate(
            [first_part.reshape(members, -1), second_part.reshape(members, -1)], axis=1
        )

    def parted(flat):
        return (flat[:, :cut].reshape(shard_gu.shape), flat[:, cut:].reshape(shard_dn.shape))

    own_source = winner[member_index]

    def take_root(root, carry):
        sent_gu, sent_dn = (spread(shard_gu, "member", root), spread(shard_dn, "member", root))
        wanted = own_source == root
        return (jnp.where(wanted, sent_gu, carry[0]), jnp.where(wanted, sent_dn, carry[1]))

    copied_gu, copied_dn = lax.fori_loop(0, members, take_root, (shard_gu, shard_dn))
    first_gu, first_dn = parted(
        lax.all_to_all(
            jnp.take(
                lax.all_to_all(
                    joined(mom1_gate_up[0], mom1_down[0]).astype(jnp.bfloat16),
                    "member",
                    split_axis=0,
                    concat_axis=0,
                    tiled=True,
                ).astype(jnp.float32),
                winner,
                axis=0,
            ).astype(jnp.bfloat16),
            "member",
            split_axis=0,
            concat_axis=0,
            tiled=True,
        ).astype(jnp.float32)
    )
    second_gu, second_dn = parted(
        lax.all_to_all(
            jnp.take(
                lax.all_to_all(
                    joined(mom2_gate_up[0], mom2_down[0]).astype(jnp.bfloat16),
                    "member",
                    split_axis=0,
                    concat_axis=0,
                    tiled=True,
                ).astype(jnp.float32),
                winner,
                axis=0,
            ).astype(jnp.bfloat16),
            "member",
            split_axis=0,
            concat_axis=0,
            tiled=True,
        ).astype(jnp.float32)
    )
    rate = learning[winner[member_index]]
    columns = rows_in
    preact = jnp.dot(
        columns,
        lax.all_gather(copied_gu, "fsdp", axis=0, tiled=True),
        preferred_element_type=jnp.float32,
    ) * width ** (-0.5)
    gate = preact[:, :units]
    upper = preact[:, units:]
    sigma = jax.nn.sigmoid(gate)
    active = gate * sigma
    hidden = (active * upper).astype(jnp.bfloat16)
    dhidden = lax.dot_general(
        upstream,
        lax.all_gather(copied_dn, "fsdp", axis=0, tiled=True),
        (((1,), (1,)), ((), ())),
        preferred_element_type=jnp.float32,
    ) * units ** (-0.5)
    dgate = dhidden * upper * (sigma * (1.0 + gate * (1.0 - sigma)))
    dupper = dhidden * active
    dpreact = (jnp.concatenate([dgate, dupper], axis=1) * width ** (-0.5)).astype(jnp.bfloat16)
    columns = rows_in
    grad_gu = lax.psum_scatter(
        lax.dot_general(
            columns, dpreact, (((0,), (0,)), ((), ())), preferred_element_type=jnp.float32
        ).astype(jnp.bfloat16),
        "fsdp",
        scatter_dimension=0,
        tiled=True,
    ).astype(jnp.float32)
    columns = hidden
    product = lax.dot_general(
        columns, upstream, (((0,), (0,)), ((), ())), preferred_element_type=jnp.float32
    )
    grad_dn = lax.psum_scatter(
        (product * units ** (-0.5)).astype(jnp.bfloat16), "fsdp", scatter_dimension=0, tiled=True
    ).astype(jnp.float32)
    new_gu, new_first_gu, new_second_gu = adamw(copied_gu, grad_gu, first_gu, second_gu, rate)
    new_dn, new_first_dn, new_second_dn = adamw(copied_dn, grad_dn, first_dn, second_dn, rate)
    return (
        new_gu[None],
        new_dn[None],
        new_first_gu[None],
        new_second_gu[None],
        new_first_dn[None],
        new_second_dn[None],
    )


def one_source_ring(chunk_count, stagger, own_chunk, distance, members):
    ring = [(i, (i + 1) % members) for i in range(members)]
    got = []
    for step in range(chunk_count + stagger * (members - 2)):
        if step < stagger:
            send = own_chunk(step)
        elif step < chunk_count:
            send = jnp.where(distance == 0, own_chunk(step), got[step - stagger])
        else:
            send = got[step - stagger]
        got.append(lax.ppermute(send, "member", ring))
    return got


def blocks_of(rows, cols):
    return rows.reshape(rows.shape[0], -1, cols).transpose(1, 0, 2).reshape(-1, cols)


def rows_of(blocks, count):
    return blocks.reshape(-1, count, blocks.shape[1]).transpose(1, 0, 2).reshape(count, -1)


def on_device_four(
    tokens,
    grad_out,
    gate_up,
    down,
    mom1_gate_up,
    mom2_gate_up,
    mom1_down,
    mom2_down,
    learning,
    winner,
):
    f32 = jnp.float32
    bf16 = jnp.bfloat16
    members = lax.axis_size("member")
    member_index = lax.axis_index("member")
    fsdp_index = lax.axis_index("fsdp")
    chip = fsdp_index // 2
    core = fsdp_index % 2
    over_x = [(0, 2), (2, 0), (1, 3), (3, 1)]
    over_core = [(0, 1), (1, 0), (2, 3), (3, 2)]
    rows_in = tokens[0]
    upstream = grad_out[0]
    shard_gu = gate_up[0]
    shard_dn = down[0]
    count, width = rows_in.shape
    half = width // 2
    units = gate_up.shape[2] // 2
    rows_gu, cols = shard_gu.shape
    rows_dn = shard_dn.shape[0]
    total = rows_gu + shard_dn.size // cols

    mine = winner[member_index]
    keep = mine == member_index
    others = jnp.where(winner != jnp.arange(members, dtype=winner.dtype), winner, -1)
    source = jnp.maximum(jnp.max(others), 0)
    distance = lax.rem(member_index - source + members, members)
    rate = learning[mine]

    def my_half(x):
        return lax.dynamic_slice_in_dim(x, chip * half, half, axis=1)

    def their_half(x):
        return lax.dynamic_slice_in_dim(x, (1 - chip) * half, half, axis=1)

    dn_mine = my_half(shard_dn)
    dn_near = lax.ppermute(their_half(shard_dn), "fsdp", over_x)
    tok_mine = my_half(rows_in)
    tok_near = lax.ppermute(their_half(rows_in), "fsdp", over_x)
    up_mine = my_half(upstream)
    up_near = lax.ppermute(their_half(upstream), "fsdp", over_x)

    dn_pair = jnp.where(
        chip == 0, jnp.concatenate([dn_mine, dn_near]), jnp.concatenate([dn_near, dn_mine])
    )
    dn_blocks = blocks_of(dn_pair, cols)
    w_chunks = 4
    m_chunks = 8
    w_rows = total // w_chunks
    m_rows = total // m_chunks
    stagger = 2

    def cut(first, second, start, stop):
        parts = []
        if start < rows_gu:
            parts.append(first[start : min(stop, rows_gu)])
        if stop > rows_gu:
            parts.append(second[max(start - rows_gu, 0) : stop - rows_gu])
        return parts[0] if len(parts) == 1 else jnp.concatenate(parts)

    m1_blocks = blocks_of(mom1_down[0], cols)
    m2_blocks = blocks_of(mom2_down[0], cols)

    def own_chunk(c):
        if c < w_chunks:
            return cut(shard_gu, dn_blocks, c * w_rows, (c + 1) * w_rows)
        c -= w_chunks
        at = (c * m_rows, (c + 1) * m_rows)
        return jnp.concatenate(
            [cut(mom1_gate_up[0], m1_blocks, *at), cut(mom2_gate_up[0], m2_blocks, *at)]
        ).astype(bf16)

    chunks = w_chunks + m_chunks
    got = one_source_ring(chunks, stagger, own_chunk, distance, members)

    def arrived(c):
        value = got[c]
        for hop in range(1, members - 1):
            value = jnp.where(distance == hop + 1, got[c + stagger * hop], value)
        return value

    weights = [jnp.where(keep, own_chunk(c), arrived(c)) for c in range(w_chunks)]
    cut_chunk = rows_gu // w_rows
    at = rows_gu - cut_chunk * w_rows
    copied_gu = jnp.concatenate(weights[:cut_chunk] + [weights[cut_chunk][:at]])
    copied_dn_blocks = jnp.concatenate([weights[cut_chunk][at:]] + weights[cut_chunk + 1 :])
    copied_dn_pair = rows_of(copied_dn_blocks, 2 * rows_dn)

    mate_gu = lax.ppermute(copied_gu, "fsdp", over_core)
    gu_half = jnp.where(
        core == 0,
        jnp.concatenate([copied_gu, mate_gu]),
        jnp.concatenate([mate_gu, copied_gu]),
    )
    mate_dn = lax.ppermute(copied_dn_pair, "fsdp", over_core)
    both = jnp.stack([copied_dn_pair, mate_dn]).reshape(2, 2, rows_dn, half)
    both = jnp.where(core == 0, both, both[::-1])
    dn_half = both.transpose(1, 0, 2, 3).reshape(units, half)
    dn_there = lax.dynamic_slice_in_dim(copied_dn_pair, (1 - chip) * rows_dn, rows_dn, axis=0)
    dn_here = lax.dynamic_slice_in_dim(copied_dn_pair, chip * rows_dn, rows_dn, axis=0)
    dn_back = lax.ppermute(dn_there, "fsdp", over_x)

    def joined(here, back):
        return jnp.where(
            chip == 0,
            jnp.concatenate([here, back], axis=1),
            jnp.concatenate([back, here], axis=1),
        )

    copied_dn = joined(dn_here, dn_back)

    tok = jnp.concatenate([tok_mine, tok_near])
    up = jnp.concatenate([up_mine, up_near])
    part = jnp.concatenate(
        [
            jnp.dot(tok, gu_half, preferred_element_type=f32),
            lax.dot_general(up, dn_half, (((1,), (1,)), ((), ())), preferred_element_type=f32),
        ],
        axis=1,
    )
    near = lax.ppermute(part, "fsdp", over_x)
    whole = part + jnp.concatenate([near[count:], near[:count]])
    gate = whole[:, :units] * width ** (-0.5)
    upper = whole[:, units : 2 * units] * width ** (-0.5)
    dhidden = whole[:, 2 * units :] * units ** (-0.5)
    sigma = jax.nn.sigmoid(gate)
    active = gate * sigma
    hidden = (active * upper).astype(bf16)
    dgate = dhidden * upper * (sigma * (1.0 + gate * (1.0 - sigma)))
    dupper = dhidden * active
    dpreact = (jnp.concatenate([dgate, dupper], axis=1) * width ** (-0.5)).astype(bf16)

    half_gu = lax.dot_general(
        tok, dpreact, (((0,), (0,)), ((), ())), preferred_element_type=f32
    )
    for_mate = lax.dynamic_slice_in_dim(half_gu, (1 - core) * rows_gu, rows_gu, axis=0)
    for_me = lax.dynamic_slice_in_dim(half_gu, core * rows_gu, rows_gu, axis=0)
    grad_gu = for_me + lax.ppermute(for_mate.astype(bf16), "fsdp", over_core).astype(f32)
    half_dn = lax.dot_general(
        hidden, up, (((0,), (0,)), ((), ())), preferred_element_type=f32
    ) * units ** (-0.5)
    half_dn = half_dn.reshape(2, 2, rows_dn, half)
    dn_for_mate = lax.dynamic_index_in_dim(half_dn, 1 - core, axis=1, keepdims=False)
    dn_for_me = lax.dynamic_index_in_dim(half_dn, core, axis=1, keepdims=False)
    pair_dn = dn_for_me + lax.ppermute(dn_for_mate.astype(bf16), "fsdp", over_core).astype(f32)
    grad_there = lax.dynamic_index_in_dim(pair_dn, 1 - chip, axis=0, keepdims=False)
    grad_here = lax.dynamic_index_in_dim(pair_dn, chip, axis=0, keepdims=False)
    grad_back = lax.ppermute(grad_there.astype(bf16), "fsdp", over_x).astype(f32)
    grad_dn = joined(grad_here, grad_back)

    came = [arrived(c) for c in range(w_chunks, chunks)]
    first = jnp.concatenate([p[:m_rows] for p in came])
    second = jnp.concatenate([p[m_rows:] for p in came])
    first_gu = jnp.where(keep, mom1_gate_up[0], first[:rows_gu].astype(f32))
    second_gu = jnp.where(keep, mom2_gate_up[0], second[:rows_gu].astype(f32))
    first_dn = jnp.where(keep, mom1_down[0], rows_of(first[rows_gu:], rows_dn).astype(f32))
    second_dn = jnp.where(keep, mom2_down[0], rows_of(second[rows_gu:], rows_dn).astype(f32))
    new_gu, new_first_gu, new_second_gu = adamw(copied_gu, grad_gu, first_gu, second_gu, rate)
    new_dn, new_first_dn, new_second_dn = adamw(copied_dn, grad_dn, first_dn, second_dn, rate)
    return (
        new_gu[None],
        new_dn[None],
        new_first_gu[None],
        new_second_gu[None],
        new_first_dn[None],
        new_second_dn[None],
    )


def solution(mesh):
    small = mesh.shape["member"] == 4 and mesh.shape["fsdp"] == 4
    return jax.shard_map(
        on_device_four if small else on_device_any,
        mesh=mesh,
        in_specs=(
            P(("groups", "member"), "fsdp", None),
            P(("groups", "member"), "fsdp", None),
            P(("groups", "member"), "fsdp", None),
            P(("groups", "member"), "fsdp", None),
            P(("groups", "member"), "fsdp", None),
            P(("groups", "member"), "fsdp", None),
            P(("groups", "member"), "fsdp", None),
            P(("groups", "member"), "fsdp", None),
            P("groups"),
            P("groups"),
        ),
        out_specs=(
            P(("groups", "member"), "fsdp", None),
            P(("groups", "member"), "fsdp", None),
            P(("groups", "member"), "fsdp", None),
            P(("groups", "member"), "fsdp", None),
            P(("groups", "member"), "fsdp", None),
            P(("groups", "member"), "fsdp", None),
        ),
        check_vma=False,
    )
```

```python
import functools

import jax
import jax.numpy as jnp
from jax import lax
from jax.experimental import pallas as pl
from jax.experimental.pallas import tpu as pltpu
from jax.sharding import PartitionSpec as P

beta_one = 0.9
beta_two = 0.95
epsilon = 1e-08
decay = 0.1


def spread(block, axis, source):
    block = jnp.where(lax.axis_index(axis) == source, block, jnp.zeros_like(block))
    return lax.psum(block, axis)


def adamw(weight, grad, first, second, rate):
    first_new = beta_one * first + (1.0 - beta_one) * grad
    second_new = beta_two * second + (1.0 - beta_two) * grad * grad
    wide = weight.astype(jnp.float32)
    updated = wide - rate * (first_new / (jnp.sqrt(second_new) + epsilon) + decay * wide)
    return (updated.astype(jnp.bfloat16), first_new, second_new)


def on_device_any(
    tokens,
    grad_out,
    gate_up,
    down,
    mom1_gate_up,
    mom2_gate_up,
    mom1_down,
    mom2_down,
    learning,
    winner,
):
    members = lax.axis_size("member")
    member_index = lax.axis_index("member")
    rows_in = tokens[0]
    upstream = grad_out[0]
    width = rows_in.shape[1]
    units = gate_up.shape[2] // 2
    shard_gu = gate_up[0]
    shard_dn = down[0]
    cut = shard_gu.size // members

    def joined(first_part, second_part):
        return jnp.concatenate(
            [first_part.reshape(members, -1), second_part.reshape(members, -1)], axis=1
        )

    def parted(flat):
        return (flat[:, :cut].reshape(shard_gu.shape), flat[:, cut:].reshape(shard_dn.shape))

    own_source = winner[member_index]

    def take_root(root, carry):
        sent_gu, sent_dn = (spread(shard_gu, "member", root), spread(shard_dn, "member", root))
        wanted = own_source == root
        return (jnp.where(wanted, sent_gu, carry[0]), jnp.where(wanted, sent_dn, carry[1]))

    copied_gu, copied_dn = lax.fori_loop(0, members, take_root, (shard_gu, shard_dn))
    first_gu, first_dn = parted(
        lax.all_to_all(
            jnp.take(
                lax.all_to_all(
                    joined(mom1_gate_up[0], mom1_down[0]).astype(jnp.bfloat16),
                    "member",
                    split_axis=0,
                    concat_axis=0,
                    tiled=True,
                ).astype(jnp.float32),
                winner,
                axis=0,
            ).astype(jnp.bfloat16),
            "member",
            split_axis=0,
            concat_axis=0,
            tiled=True,
        ).astype(jnp.float32)
    )
    second_gu, second_dn = parted(
        lax.all_to_all(
            jnp.take(
                lax.all_to_all(
                    joined(mom2_gate_up[0], mom2_down[0]).astype(jnp.bfloat16),
                    "member",
                    split_axis=0,
                    concat_axis=0,
                    tiled=True,
                ).astype(jnp.float32),
                winner,
                axis=0,
            ).astype(jnp.bfloat16),
            "member",
            split_axis=0,
            concat_axis=0,
            tiled=True,
        ).astype(jnp.float32)
    )
    rate = learning[winner[member_index]]
    columns = rows_in
    preact = jnp.dot(
        columns,
        lax.all_gather(copied_gu, "fsdp", axis=0, tiled=True),
        preferred_element_type=jnp.float32,
    ) * width ** (-0.5)
    gate = preact[:, :units]
    upper = preact[:, units:]
    sigma = jax.nn.sigmoid(gate)
    active = gate * sigma
    hidden = (active * upper).astype(jnp.bfloat16)
    dhidden = lax.dot_general(
        upstream,
        lax.all_gather(copied_dn, "fsdp", axis=0, tiled=True),
        (((1,), (1,)), ((), ())),
        preferred_element_type=jnp.float32,
    ) * units ** (-0.5)
    dgate = dhidden * upper * (sigma * (1.0 + gate * (1.0 - sigma)))
    dupper = dhidden * active
    dpreact = (jnp.concatenate([dgate, dupper], axis=1) * width ** (-0.5)).astype(jnp.bfloat16)
    columns = rows_in
    grad_gu = lax.psum_scatter(
        lax.dot_general(
            columns, dpreact, (((0,), (0,)), ((), ())), preferred_element_type=jnp.float32
        ).astype(jnp.bfloat16),
        "fsdp",
        scatter_dimension=0,
        tiled=True,
    ).astype(jnp.float32)
    columns = hidden
    product = lax.dot_general(
        columns, upstream, (((0,), (0,)), ((), ())), preferred_element_type=jnp.float32
    )
    grad_dn = lax.psum_scatter(
        (product * units ** (-0.5)).astype(jnp.bfloat16), "fsdp", scatter_dimension=0, tiled=True
    ).astype(jnp.float32)
    new_gu, new_first_gu, new_second_gu = adamw(copied_gu, grad_gu, first_gu, second_gu, rate)
    new_dn, new_first_dn, new_second_dn = adamw(copied_dn, grad_dn, first_dn, second_dn, rate)
    return (
        new_gu[None],
        new_dn[None],
        new_first_gu[None],
        new_second_gu[None],
        new_first_dn[None],
        new_second_dn[None],
    )


ANY = pl.BlockSpec(memory_space=pl.ANY)
SMEM = pl.BlockSpec(memory_space=pltpu.SMEM)
VMEM = pl.BlockSpec(memory_space=pltpu.VMEM)
BIG = pltpu.CompilerParams(vmem_limit_bytes=48 * 1024 * 1024)
STAGGER = 2
W_CHUNKS = 4
M_CHUNKS = 8
CHUNKS = W_CHUNKS + M_CHUNKS


def cost(flops, moved):
    return pl.CostEstimate(flops=flops, bytes_accessed=moved, transcendentals=0)


def after(value, *others):
    return lax.optimization_barrier((value,) + others)[0]


def pick(where, pieces, got):
    def kernel(where_ref, got_ref, *refs):
        own, out, sems = refs[: len(pieces)], refs[len(pieces)], refs[len(pieces) + 1]

        @pl.when(where_ref[0] == 0)
        def _():
            copies = [
                pltpu.make_async_copy(ref.at[index], out.at[pl.ds(*rows)], sems.at[n])
                for n, (ref, (_, index, rows)) in enumerate(zip(own, pieces))
            ]
            for copy in copies:
                copy.start()
            for copy in copies:
                copy.wait()

    return pl.pallas_call(
        kernel,
        out_shape=jax.ShapeDtypeStruct(got.shape, got.dtype),
        in_specs=[SMEM, ANY] + [ANY] * len(pieces),
        out_specs=ANY,
        scratch_shapes=[pltpu.SemaphoreType.DMA((len(pieces),))],
        input_output_aliases={1: 0},
        cost_estimate=cost(0, got.size * 2),
        name="pick",
    )(where, got, *[array for array, _, _ in pieces])


def assemble(mode, own, pieces, out_shape):
    hops = len(pieces[0][0])
    flat = [array for arrays, _, _, _ in pieces for array in arrays]

    def kernel(mode_ref, own_ref, *refs):
        out, sems = refs[len(flat)], refs[len(flat) + 1]

        @pl.when(mode_ref[0] == 0)
        def _():
            copy = pltpu.make_async_copy(own_ref, out, sems.at[0])
            copy.start()
            copy.wait()

        for hop in range(hops):

            @pl.when(mode_ref[0] == hop + 1)
            def _():
                copies = [
                    pltpu.make_async_copy(
                        refs[n * hops + hop].at[pl.ds(start, rows)],
                        out.at[pl.ds(to, rows)],
                        sems.at[n],
                    )
                    for n, (_, start, rows, to) in enumerate(pieces)
                ]
                for copy in copies:
                    copy.start()
                for copy in copies:
                    copy.wait()

    return pl.pallas_call(
        kernel,
        out_shape=jax.ShapeDtypeStruct(out_shape, own.dtype),
        in_specs=[SMEM, ANY] + [ANY] * len(flat),
        out_specs=ANY,
        scratch_shapes=[pltpu.SemaphoreType.DMA((len(pieces),))],
        cost_estimate=cost(0, own.size * 4),
        name="assemble",
    )(mode, own, *flat)


def pack_moments(m1_gu, m2_gu, m1_dn, m2_dn):
    _, rows_gu, cols = m1_gu.shape
    _, rows_dn, width = m1_dn.shape
    part = rows_gu // M_CHUNKS
    blocks = width // cols // M_CHUNKS
    each = part + blocks * rows_dn
    steps = 4
    per = M_CHUNKS // steps

    def kernel(m1g, m2g, m1d, m2d, out):
        for n in range(per):
            for base, gu, dn in ((0, m1g, m1d), (each, m2g, m2d)):
                out[n, base : base + part] = gu[0, n * part : (n + 1) * part].astype(out.dtype)
                for b in range(blocks):
                    at = (n * blocks + b) * cols
                    to = base + part + b * rows_dn
                    out[n, to : to + rows_dn] = dn[0, :, at : at + cols].astype(out.dtype)

    gu_spec = pl.BlockSpec((1, per * part, cols), lambda i: (0, i, 0))
    dn_spec = pl.BlockSpec((1, rows_dn, width // steps), lambda i: (0, 0, i))
    return pl.pallas_call(
        kernel,
        grid=(steps,),
        out_shape=jax.ShapeDtypeStruct((M_CHUNKS, 2 * each, cols), jnp.bfloat16),
        in_specs=[gu_spec, gu_spec, dn_spec, dn_spec],
        out_specs=pl.BlockSpec((per, 2 * each, cols), lambda i: (i, 0, 0)),
        cost_estimate=cost(0, 12 * (m1_gu.size + m1_dn.size)),
        name="pack_moments",
    )(m1_gu, m2_gu, m1_dn, m2_dn)


def swap_blocks(place, down, near, cols):
    _, rows, width = down.shape
    half = width // 2
    blocks = half // cols

    def kernel(place_ref, down_ref, near_ref, out, buf, sem):
        chip = place_ref[0]
        copy = pltpu.make_async_copy(
            down_ref.at[0, :, pl.ds(pl.multiple_of(chip * half, half), half)], buf, sem
        )
        copy.start()
        for b in range(blocks):
            out[b, 1 - chip] = near_ref[:, b * cols : (b + 1) * cols]
        copy.wait()
        for b in range(blocks):
            out[b, chip] = buf[:, b * cols : (b + 1) * cols]

    return pl.pallas_call(
        kernel,
        out_shape=jax.ShapeDtypeStruct((blocks, 2, rows, cols), down.dtype),
        in_specs=[SMEM, ANY, VMEM],
        out_specs=VMEM,
        scratch_shapes=[pltpu.VMEM((rows, half), down.dtype), pltpu.SemaphoreType.DMA],
        cost_estimate=cost(0, down.size * 4),
        name="swap_blocks",
    )(place, down, near)


def forward(place, tokens, tok_near, grad_out, up_near, gu, gu_mate, dn, dn_mate):
    _, count, width = tokens.shape
    half = width // 2
    rows, cols = gu.shape
    blocks, _, rows_dn, _ = dn.shape
    units = 4 * rows_dn

    def kernel(place_ref, tok_r, tokn_r, up_r, upn_r, gu_r, gum_r, dn_r, dnm_r, out, sent, tok, up, gub, dnb, sems):
        chip, core = place_ref[0], place_ref[1]
        mine = pl.ds(pl.multiple_of(chip * half, half), half)
        first = pl.ds(pl.multiple_of(core * rows, rows), rows)
        second = pl.ds(pl.multiple_of((1 - core) * rows, rows), rows)
        pairs = [
            (gu_r, gub.at[first]),
            (gum_r, gub.at[second]),
            (tok_r.at[0, :, mine], tok.at[pl.ds(0, count)]),
            (tokn_r, tok.at[pl.ds(count, count)]),
            (dn_r, dnb.at[:, :, core]),
            (dnm_r, dnb.at[:, :, 1 - core]),
            (up_r.at[0, :, mine], up.at[pl.ds(0, count)]),
            (upn_r, up.at[pl.ds(count, count)]),
        ]
        copies = [pltpu.make_async_copy(a, b, sems.at[n]) for n, (a, b) in enumerate(pairs)]
        for copy in copies:
            copy.start()
        for copy in copies[:4]:
            copy.wait()
        pre = jnp.dot(tok[...], gub[...], preferred_element_type=jnp.float32)
        out[:, :cols] = pre
        sent[:, :cols] = pre.astype(sent.dtype)
        for copy in copies[4:]:
            copy.wait()
        dh = jnp.zeros((2 * count, units), jnp.float32)
        for b in range(blocks):
            dh += lax.dot_general(
                up[:, b * cols : (b + 1) * cols],
                dnb[b].reshape(units, cols),
                (((1,), (1,)), ((), ())),
                preferred_element_type=jnp.float32,
            )
        out[:, cols:] = dh
        sent[:, cols:] = dh.astype(sent.dtype)

    shape = (2 * count, cols + units)
    return pl.pallas_call(
        kernel,
        out_shape=(
            jax.ShapeDtypeStruct(shape, jnp.float32),
            jax.ShapeDtypeStruct(shape, jnp.bfloat16),
        ),
        in_specs=[SMEM] + [ANY] * 8,
        out_specs=(VMEM, VMEM),
        scratch_shapes=[
            pltpu.VMEM((2 * count, half), jnp.bfloat16),
            pltpu.VMEM((2 * count, half), jnp.bfloat16),
            pltpu.VMEM((half, cols), jnp.bfloat16),
            pltpu.VMEM((blocks, 2, 2, rows_dn, cols), jnp.bfloat16),
            pltpu.SemaphoreType.DMA((8,)),
        ],
        compiler_params=BIG,
        cost_estimate=cost(4 * count * half * shape[1], 5 * 1024 * 1024),
        name="forward",
    )(place, tokens, tok_near, grad_out, up_near, gu, gu_mate, dn, dn_mate)


def backward(place, part, near, tokens, tok_near, grad_out, up_near, rows, rows_dn):
    _, count, width = tokens.shape
    half = width // 2
    units = 4 * rows_dn
    cols = 2 * units
    blocks = half // cols

    def kernel(place_ref, part_r, near_r, tok_r, tokn_r, up_r, upn_r, g_own, g_mate, d_own, d_mate, tok, tokm, up, res, sems):
        chip, core = place_ref[0], place_ref[1]
        mine = pl.ds(pl.multiple_of(chip * half, half), half)
        first = pl.multiple_of(core * rows, rows)
        second = pl.multiple_of((1 - core) * rows, rows)
        here = pl.multiple_of(chip * half, half)
        pairs = [
            (up_r.at[0, :, mine], up.at[pl.ds(0, count)]),
            (upn_r, up.at[pl.ds(count, count)]),
            (tok_r.at[0, :, pl.ds(here + second, rows)], tokm.at[pl.ds(0, count)]),
            (tokn_r.at[:, pl.ds(second, rows)], tokm.at[pl.ds(count, count)]),
            (tok_r.at[0, :, pl.ds(here + first, rows)], tok.at[pl.ds(0, count)]),
            (tokn_r.at[:, pl.ds(first, rows)], tok.at[pl.ds(count, count)]),
        ]
        copies = [pltpu.make_async_copy(a, b, sems.at[n]) for n, (a, b) in enumerate(pairs)]
        for copy in copies:
            copy.start()
        other = jnp.concatenate([near_r[count:], near_r[:count]]).astype(jnp.float32)
        whole = part_r[...] + other
        gate = whole[:, :units] * width ** (-0.5)
        upper = whole[:, units:cols] * width ** (-0.5)
        dhidden = whole[:, cols:] * units ** (-0.5)
        sigma = jax.nn.sigmoid(gate)
        active = gate * sigma
        hidden = (active * upper).astype(jnp.bfloat16)
        dgate = dhidden * upper * (sigma * (1.0 + gate * (1.0 - sigma)))
        dupper = dhidden * active
        dpre = (jnp.concatenate([dgate, dupper], axis=1) * width ** (-0.5)).astype(jnp.bfloat16)
        over_tokens = (((0,), (0,)), ((), ()))
        copies[0].wait()
        copies[1].wait()
        for b in range(blocks):
            res[b] = lax.dot_general(
                hidden, up[:, b * cols : (b + 1) * cols], over_tokens, preferred_element_type=jnp.float32
            ) * units ** (-0.5)
        for b in range(blocks):
            for x in range(2):
                base = x * 2 * rows_dn
                d_own[b, x] = res[b, pl.ds(pl.multiple_of(base + core * rows_dn, rows_dn), rows_dn)]
                d_mate[b, x] = res[
                    b, pl.ds(pl.multiple_of(base + (1 - core) * rows_dn, rows_dn), rows_dn)
                ].astype(d_mate.dtype)
        copies[2].wait()
        copies[3].wait()
        g_mate[...] = lax.dot_general(
            tokm[...], dpre, over_tokens, preferred_element_type=jnp.float32
        ).astype(g_mate.dtype)
        copies[4].wait()
        copies[5].wait()
        g_own[...] = lax.dot_general(tok[...], dpre, over_tokens, preferred_element_type=jnp.float32)

    f32, bf16 = jnp.float32, jnp.bfloat16
    dn_shape = (blocks, 2, rows_dn, cols)
    return pl.pallas_call(
        kernel,
        out_shape=(
            jax.ShapeDtypeStruct((rows, cols), f32),
            jax.ShapeDtypeStruct((rows, cols), bf16),
            jax.ShapeDtypeStruct(dn_shape, f32),
            jax.ShapeDtypeStruct(dn_shape, bf16),
        ),
        in_specs=[SMEM, VMEM, VMEM] + [ANY] * 4,
        out_specs=(VMEM,) * 4,
        scratch_shapes=[
            pltpu.VMEM((2 * count, rows), bf16),
            pltpu.VMEM((2 * count, rows), bf16),
            pltpu.VMEM((2 * count, half), bf16),
            pltpu.VMEM((blocks, units, cols), f32),
            pltpu.SemaphoreType.DMA((6,)),
        ],
        compiler_params=BIG,
        cost_estimate=cost(4 * count * half * (cols + units), 6 * 1024 * 1024),
        name="backward",
    )(place, part, near, tokens, tok_near, grad_out, up_near)


def update(place, rate, moments, came, gu, dn, dn_back, grads):
    m1_gu, m2_gu, m1_dn, m2_dn = moments
    _, rows_gu, cols = m1_gu.shape
    _, rows_dn, width = m1_dn.shape
    blocks = width // cols
    half_blocks = blocks // 2
    part = rows_gu // M_CHUNKS
    per = blocks // M_CHUNKS
    each = part + per * rows_dn
    hops = len(came[0])
    flat = [array for arrays in came for array in arrays]
    f32, bf16 = jnp.float32, jnp.bfloat16

    def kernel(place_ref, rate_ref, *refs):
        m1g, m2g, m1d, m2d = refs[:4]
        arrived = refs[4 : 4 + len(flat)]
        gu_r, dn_r, back_r, go_r, gm_r, do_r, dm_r, gb_r = refs[4 + len(flat) : 12 + len(flat)]
        ngu, ndn, n1g, n2g, n1d, n2d = refs[12 + len(flat) : 18 + len(flat)]
        (bgu, bdn, bgo, bgm, bdo, bdm, bgb, gdn, own_g, own_d, moved, ogu, odn, o1g, o2g, o1d, o2d, sems, msems, osems) = refs[18 + len(flat) :]
        chip, mode = place_ref[0], place_ref[2]
        factor = rate_ref[0]
        pairs = [
            (gu_r, bgu),
            (dn_r.at[:, chip], bdn.at[chip]),
            (back_r, bdn.at[1 - chip]),
            (go_r, bgo),
            (gm_r, bgm),
            (do_r.at[:, chip], bdo),
            (dm_r.at[:, chip], bdm),
            (gb_r, bgb),
        ]
        copies = [pltpu.make_async_copy(a, b, sems.at[n]) for n, (a, b) in enumerate(pairs)]
        for copy in copies:
            copy.start()

        def own_copies(j):
            g, d = pl.ds(j * part, part), pl.ds(j * per * cols, per * cols)
            return [
                pltpu.make_async_copy(m1g.at[0, g], own_g.at[0, g], msems.at[j, 0]),
                pltpu.make_async_copy(m2g.at[0, g], own_g.at[1, g], msems.at[j, 1]),
                pltpu.make_async_copy(m1d.at[0, :, d], own_d.at[0, :, d], msems.at[j, 2]),
                pltpu.make_async_copy(m2d.at[0, :, d], own_d.at[1, :, d], msems.at[j, 3]),
            ]

        def moved_copy(j, hop):
            return pltpu.make_async_copy(arrived[j * hops + hop], moved.at[j], msems.at[j, 0])

        @pl.when(mode == 0)
        def _():
            for j in range(M_CHUNKS):
                for copy in own_copies(j):
                    copy.start()

        for hop in range(hops):

            @pl.when(mode == hop + 1)
            def _():
                for j in range(M_CHUNKS):
                    moved_copy(j, hop).start()

        for copy in copies:
            copy.wait()
        gdn[chip] = bdo[...] + bdm[...].astype(f32)
        gdn[1 - chip] = bgb[...].astype(f32)

        def step(weight, grad, first, second):
            first_new = beta_one * first + (1.0 - beta_one) * grad
            second_new = beta_two * second + (1.0 - beta_two) * grad * grad
            wide = weight.astype(f32)
            updated = wide - factor * (first_new / (jnp.sqrt(second_new) + epsilon) + decay * wide)
            return updated.astype(bf16), first_new, second_new

        outs = []
        for j in range(M_CHUNKS):

            @pl.when(mode == 0)
            def _():
                for copy in own_copies(j):
                    copy.wait()

            @pl.when(mode != 0)
            def _():
                moved_copy(j, 0).wait()

            def moment(n, own, base, size):
                there = moved[j, n * each + base : n * each + base + size].astype(f32)
                return jnp.where(mode == 0, own, there)

            g = slice(j * part, (j + 1) * part)
            first = moment(0, own_g[0, g], 0, part)
            second = moment(1, own_g[1, g], 0, part)
            grad = bgo[g] + bgm[g].astype(f32)
            ogu[g], o1g[g], o2g[g] = step(bgu[g], grad, first, second)
            for i in range(per):
                b = j * per + i
                at = slice(b * cols, (b + 1) * cols)
                base = part + i * rows_dn
                first = moment(0, own_d[0, :, at], base, rows_dn)
                second = moment(1, own_d[1, :, at], base, rows_dn)
                h, n = divmod(b, half_blocks)
                odn[:, at], o1d[:, at], o2d[:, at] = step(bdn[h, n], gdn[h, n], first, second)
            gs, ds = pl.ds(j * part, part), pl.ds(j * per * cols, per * cols)
            for n, (a, b) in enumerate(
                (
                    (ogu.at[gs], ngu.at[0, gs]),
                    (o1g.at[gs], n1g.at[0, gs]),
                    (o2g.at[gs], n2g.at[0, gs]),
                    (odn.at[:, ds], ndn.at[0, :, ds]),
                    (o1d.at[:, ds], n1d.at[0, :, ds]),
                    (o2d.at[:, ds], n2d.at[0, :, ds]),
                )
            ):
                copy = pltpu.make_async_copy(a, b, osems.at[j, n])
                copy.start()
                outs.append(copy)
        for copy in outs:
            copy.wait()

    gu_shape, dn_shape = (rows_gu, cols), (rows_dn, width)
    side = (half_blocks, rows_dn, cols)
    shapes = [gu_shape, dn_shape, gu_shape, gu_shape, dn_shape, dn_shape]
    types = [bf16, bf16, f32, f32, f32, f32]
    return pl.pallas_call(
        kernel,
        out_shape=tuple(jax.ShapeDtypeStruct((1,) + s, t) for s, t in zip(shapes, types)),
        in_specs=[SMEM, SMEM] + [ANY] * (12 + len(flat)),
        out_specs=(ANY,) * 6,
        scratch_shapes=[
            pltpu.VMEM(gu_shape, bf16),
            pltpu.VMEM((2,) + side, bf16),
            pltpu.VMEM(gu_shape, f32),
            pltpu.VMEM(gu_shape, bf16),
            pltpu.VMEM(side, f32),
            pltpu.VMEM(side, bf16),
            pltpu.VMEM(side, bf16),
            pltpu.VMEM((2,) + side, f32),
            pltpu.VMEM((2,) + gu_shape, f32),
            pltpu.VMEM((2,) + dn_shape, f32),
            pltpu.VMEM((M_CHUNKS, 2 * each, cols), bf16),
        ]
        + [pltpu.VMEM(s, t) for s, t in zip(shapes, types)]
        + [
            pltpu.SemaphoreType.DMA((8,)),
            pltpu.SemaphoreType.DMA((M_CHUNKS, 4)),
            pltpu.SemaphoreType.DMA((M_CHUNKS, 6)),
        ],
        compiler_params=BIG,
        cost_estimate=cost(0, 10 * 1024 * 1024),
        name="update",
    )(place, rate, m1_gu, m2_gu, m1_dn, m2_dn, *flat, gu, dn, dn_back, *grads)


def on_device_four(
    tokens,
    grad_out,
    gate_up,
    down,
    mom1_gate_up,
    mom2_gate_up,
    mom1_down,
    mom2_down,
    learning,
    winner,
):
    bf16 = jnp.bfloat16
    members = lax.axis_size("member")
    member_index = lax.axis_index("member")
    fsdp_index = lax.axis_index("fsdp")
    chip = fsdp_index // 2
    core = fsdp_index % 2
    over_x = [(0, 2), (2, 0), (1, 3), (3, 1)]
    over_core = [(0, 1), (1, 0), (2, 3), (3, 2)]
    ring = [(i, (i + 1) % members) for i in range(members)]
    half = tokens.shape[2] // 2
    _, rows_gu, cols = gate_up.shape
    rows_dn = down.shape[1]
    rows_all = rows_gu + down.size // cols
    w_rows = rows_all // W_CHUNKS

    mine = winner[member_index]
    others = jnp.where(winner != jnp.arange(members, dtype=winner.dtype), winner, -1)
    source = jnp.maximum(jnp.max(others), 0)
    distance = lax.rem(member_index - source + members, members)
    mode = jnp.where(mine == member_index, 0, distance)
    rate = learning[mine].reshape(1)
    where = distance.astype(jnp.int32).reshape(1)
    place = jnp.stack([chip, core, mode]).astype(jnp.int32)
    mode = place[2:]

    def theirs(x):
        return lax.dynamic_slice_in_dim(x[0], (1 - chip) * half, half, axis=1)

    sent = [gate_up[0, :w_rows], gate_up[0, w_rows : 2 * w_rows]]
    got = [lax.ppermute(sent[0], "member", ring), lax.ppermute(sent[1], "member", ring)]
    down_t, tokens_t, grad_out_t = (
        after(down, *sent),
        after(tokens, *sent),
        after(grad_out, *sent),
    )
    dn_near = lax.ppermute(theirs(down_t), "fsdp", over_x)
    tok_near = lax.ppermute(theirs(tokens_t), "fsdp", over_x)
    up_near = lax.ppermute(theirs(grad_out_t), "fsdp", over_x)
    dn_blocks = swap_blocks(place, down, dn_near, cols)
    dn_rows = dn_blocks.reshape(-1, cols)
    packed = pack_moments(after(mom1_gate_up, *sent), mom2_gate_up, mom1_down, mom2_down)

    def pieces_of(c):
        if c >= W_CHUNKS:
            return [(packed, c - W_CHUNKS, (0, packed.shape[1]))]
        low, high = c * w_rows, (c + 1) * w_rows
        found = []
        if low < rows_gu:
            rows = min(high, rows_gu) - low
            found.append((gate_up, (0, pl.ds(low, rows)), (0, rows)))
        if high > rows_gu:
            begin = max(low, rows_gu)
            found.append((dn_rows, (pl.ds(begin - rows_gu, high - begin),), (begin - low, high - begin)))
        return found

    held = []
    hops = members - 1
    last = STAGGER * (hops - 1)

    def versions(c):
        return [held[c + STAGGER * hop] for hop in range(hops)]

    gap = {}
    cut = rows_gu // w_rows
    for step in range(STAGGER, CHUNKS + last + STAGGER):
        back = got[step - STAGGER]
        if step < CHUNKS:
            back = pick(where, pieces_of(step), back)
        held.append(back)
        if step < CHUNKS + last:
            got.append(lax.ppermute(back, "member", ring))
        ready = len(held) - 1 - last
        if ready == cut:
            gu_pieces = [(versions(c), 0, w_rows, c * w_rows) for c in range(cut)]
            left = rows_gu - cut * w_rows
            gu_pieces.append((versions(cut), 0, left, cut * w_rows))
            gu = assemble(mode, gate_up[0], gu_pieces, gate_up.shape[1:])
            gu_mate = lax.ppermute(gu, "fsdp", over_core)
        if ready == W_CHUNKS - 1:
            dn_pieces = [(versions(cut), left, w_rows - left, 0)]
            for c in range(cut + 1, W_CHUNKS):
                dn_pieces.append((versions(c), 0, w_rows, c * w_rows - rows_gu))
            dn_r = assemble(mode, dn_rows, dn_pieces, dn_rows.shape)
            dn_mate = lax.ppermute(dn_r, "fsdp", over_core)
            dn = dn_r.reshape(dn_blocks.shape)
            dn_there = lax.dynamic_index_in_dim(dn, 1 - chip, axis=1, keepdims=False)
            dn_back = lax.ppermute(dn_there, "fsdp", over_x)
        if ready == W_CHUNKS:
            part, part_sent = forward(
                place,
                tokens,
                tok_near,
                grad_out,
                up_near,
                after(gu, back),
                gu_mate,
                dn,
                dn_mate.reshape(dn_blocks.shape),
            )
            near = lax.ppermute(part_sent, "fsdp", over_x)
        if step == CHUNKS + STAGGER:
            g_own, g_mate, d_own, d_mate = backward(
                place, part, after(near, back), tokens, tok_near, grad_out, up_near, rows_gu, rows_dn
            )
            g_got = lax.ppermute(g_mate, "fsdp", over_core)
            d_got = lax.ppermute(d_mate, "fsdp", over_core)
            d_there = (
                lax.dynamic_index_in_dim(d_own, 1 - chip, axis=1, keepdims=False)
                + lax.dynamic_index_in_dim(d_got, 1 - chip, axis=1, keepdims=False)
            ).astype(bf16)
            d_back = lax.ppermute(d_there, "fsdp", over_x)

    return update(
        place,
        rate,
        (mom1_gate_up, mom2_gate_up, mom1_down, mom2_down),
        [versions(c) for c in range(W_CHUNKS, CHUNKS)],
        gu,
        dn,
        dn_back,
        (g_own, g_got, d_own, d_got, d_back),
    )


def solution(mesh):
    small = mesh.shape["member"] == 4 and mesh.shape["fsdp"] == 4
    return jax.shard_map(
        on_device_four if small else on_device_any,
        mesh=mesh,
        in_specs=(
            P(("groups", "member"), "fsdp", None),
            P(("groups", "member"), "fsdp", None),
            P(("groups", "member"), "fsdp", None),
            P(("groups", "member"), "fsdp", None),
            P(("groups", "member"), "fsdp", None),
            P(("groups", "member"), "fsdp", None),
            P(("groups", "member"), "fsdp", None),
            P(("groups", "member"), "fsdp", None),
            P("groups"),
            P("groups"),
        ),
        out_specs=(
            P(("groups", "member"), "fsdp", None),
            P(("groups", "member"), "fsdp", None),
            P(("groups", "member"), "fsdp", None),
            P(("groups", "member"), "fsdp", None),
            P(("groups", "member"), "fsdp", None),
            P(("groups", "member"), "fsdp", None),
        ),
        check_vma=False,
    )
```

```python
import functools

import jax
import jax.numpy as jnp
from jax import lax
from jax.experimental import pallas as pl
from jax.experimental.pallas import tpu as pltpu
from jax.sharding import PartitionSpec as P

beta_one = 0.9
beta_two = 0.95
epsilon = 1e-08
decay = 0.1


def spread(block, axis, source):
    block = jnp.where(lax.axis_index(axis) == source, block, jnp.zeros_like(block))
    return lax.psum(block, axis)


def adamw(weight, grad, first, second, rate):
    first_new = beta_one * first + (1.0 - beta_one) * grad
    second_new = beta_two * second + (1.0 - beta_two) * grad * grad
    wide = weight.astype(jnp.float32)
    updated = wide - rate * (first_new / (jnp.sqrt(second_new) + epsilon) + decay * wide)
    return (updated.astype(jnp.bfloat16), first_new, second_new)


def on_device_any(
    tokens,
    grad_out,
    gate_up,
    down,
    mom1_gate_up,
    mom2_gate_up,
    mom1_down,
    mom2_down,
    learning,
    winner,
):
    members = lax.axis_size("member")
    member_index = lax.axis_index("member")
    rows_in = tokens[0]
    upstream = grad_out[0]
    width = rows_in.shape[1]
    units = gate_up.shape[2] // 2
    shard_gu = gate_up[0]
    shard_dn = down[0]
    cut = shard_gu.size // members

    def joined(first_part, second_part):
        return jnp.concatenate(
            [first_part.reshape(members, -1), second_part.reshape(members, -1)], axis=1
        )

    def parted(flat):
        return (flat[:, :cut].reshape(shard_gu.shape), flat[:, cut:].reshape(shard_dn.shape))

    own_source = winner[member_index]

    def take_root(root, carry):
        sent_gu, sent_dn = (spread(shard_gu, "member", root), spread(shard_dn, "member", root))
        wanted = own_source == root
        return (jnp.where(wanted, sent_gu, carry[0]), jnp.where(wanted, sent_dn, carry[1]))

    copied_gu, copied_dn = lax.fori_loop(0, members, take_root, (shard_gu, shard_dn))
    first_gu, first_dn = parted(
        lax.all_to_all(
            jnp.take(
                lax.all_to_all(
                    joined(mom1_gate_up[0], mom1_down[0]).astype(jnp.bfloat16),
                    "member",
                    split_axis=0,
                    concat_axis=0,
                    tiled=True,
                ).astype(jnp.float32),
                winner,
                axis=0,
            ).astype(jnp.bfloat16),
            "member",
            split_axis=0,
            concat_axis=0,
            tiled=True,
        ).astype(jnp.float32)
    )
    second_gu, second_dn = parted(
        lax.all_to_all(
            jnp.take(
                lax.all_to_all(
                    joined(mom2_gate_up[0], mom2_down[0]).astype(jnp.bfloat16),
                    "member",
                    split_axis=0,
                    concat_axis=0,
                    tiled=True,
                ).astype(jnp.float32),
                winner,
                axis=0,
            ).astype(jnp.bfloat16),
            "member",
            split_axis=0,
            concat_axis=0,
            tiled=True,
        ).astype(jnp.float32)
    )
    rate = learning[winner[member_index]]
    columns = rows_in
    preact = jnp.dot(
        columns,
        lax.all_gather(copied_gu, "fsdp", axis=0, tiled=True),
        preferred_element_type=jnp.float32,
    ) * width ** (-0.5)
    gate = preact[:, :units]
    upper = preact[:, units:]
    sigma = jax.nn.sigmoid(gate)
    active = gate * sigma
    hidden = (active * upper).astype(jnp.bfloat16)
    dhidden = lax.dot_general(
        upstream,
        lax.all_gather(copied_dn, "fsdp", axis=0, tiled=True),
        (((1,), (1,)), ((), ())),
        preferred_element_type=jnp.float32,
    ) * units ** (-0.5)
    dgate = dhidden * upper * (sigma * (1.0 + gate * (1.0 - sigma)))
    dupper = dhidden * active
    dpreact = (jnp.concatenate([dgate, dupper], axis=1) * width ** (-0.5)).astype(jnp.bfloat16)
    columns = rows_in
    grad_gu = lax.psum_scatter(
        lax.dot_general(
            columns, dpreact, (((0,), (0,)), ((), ())), preferred_element_type=jnp.float32
        ).astype(jnp.bfloat16),
        "fsdp",
        scatter_dimension=0,
        tiled=True,
    ).astype(jnp.float32)
    columns = hidden
    product = lax.dot_general(
        columns, upstream, (((0,), (0,)), ((), ())), preferred_element_type=jnp.float32
    )
    grad_dn = lax.psum_scatter(
        (product * units ** (-0.5)).astype(jnp.bfloat16), "fsdp", scatter_dimension=0, tiled=True
    ).astype(jnp.float32)
    new_gu, new_first_gu, new_second_gu = adamw(copied_gu, grad_gu, first_gu, second_gu, rate)
    new_dn, new_first_dn, new_second_dn = adamw(copied_dn, grad_dn, first_dn, second_dn, rate)
    return (
        new_gu[None],
        new_dn[None],
        new_first_gu[None],
        new_second_gu[None],
        new_first_dn[None],
        new_second_dn[None],
    )


ANY = pl.BlockSpec(memory_space=pl.ANY)
SMEM = pl.BlockSpec(memory_space=pltpu.SMEM)
VMEM = pl.BlockSpec(memory_space=pltpu.VMEM)
STAGGER = 2
W_CHUNKS = 4
M_CHUNKS = 8
CHUNKS = W_CHUNKS + M_CHUNKS
EARLY = 5
GU_AT = 10
DN_AT = 11
BACK_AT = 13
FAR_AT = 9
SUM_AT = 15
EARLY_AT = 16


def grant(mib):
    return pltpu.CompilerParams(vmem_limit_bytes=mib * 1024 * 1024)


def cost(flops, moved):
    return pl.CostEstimate(flops=flops, bytes_accessed=moved, transcendentals=0)


def in_hbm(*arrays):
    return [pltpu.with_memory_space_constraint(array, pltpu.HBM) for array in arrays]


def in_vmem(*arrays):
    return [pltpu.with_memory_space_constraint(array, pltpu.VMEM) for array in arrays]


def after(value, *others):
    return lax.optimization_barrier((value,) + others)[0]


def mode_of(winner_ref, members):
    member = lax.axis_index("member")
    source = 0
    for other in range(members):
        source = jnp.where(winner_ref[other] != other, winner_ref[other], source)
    return jnp.where(
        winner_ref[member] == member, 0, lax.rem(member - source + members, members)
    )


def chip_and_core():
    index = lax.axis_index("fsdp")
    return index // 2, lax.rem(index, 2)


def start_all(pairs, sems):
    copies = [pltpu.make_async_copy(a, b, sems.at[n]) for n, (a, b) in enumerate(pairs)]
    for copy in copies:
        copy.start()
    return copies


def wait_all(copies):
    for copy in copies:
        copy.wait()


def assemble(winner, own, held, pieces, out_shape):
    members = winner.shape[0]
    arrays = [array for array, _, _, _ in own]

    def kernel(winner_ref, *refs):
        own_refs, came = refs[: len(own)], refs[len(own) : len(own) + len(held)]
        out, sems = refs[len(own) + len(held) :]
        mode = mode_of(winner_ref, members)

        def move(refs, places):
            wait_all(
                start_all(
                    [
                        (ref.at[pl.ds(start, rows)], out.at[pl.ds(to, rows)])
                        for ref, (_, start, rows, to) in zip(refs, places)
                    ],
                    sems,
                )
            )

        @pl.when(mode == 0)
        def _():
            move(own_refs, own)

        for hop in range(members - 1):

            @pl.when(mode == hop + 1)
            def _():
                move([came[place + STAGGER * hop] for place, _, _, _ in pieces], pieces)

    return pl.pallas_call(
        kernel,
        out_shape=jax.ShapeDtypeStruct(out_shape, jnp.bfloat16),
        in_specs=[SMEM] + [ANY] * (len(own) + len(held)),
        out_specs=VMEM,
        scratch_shapes=[pltpu.SemaphoreType.DMA((max(len(own), len(pieces)),))],
        compiler_params=grant(4),
        cost_estimate=cost(0, 4 * out_shape[0] * out_shape[1]),
        name="assemble",
    )(winner, *arrays, *held)


def pack_moments(m1_gu, m2_gu, m1_dn, m2_dn):
    _, rows_gu, cols = m1_gu.shape
    _, rows_dn, width = m1_dn.shape
    part = rows_gu // M_CHUNKS
    wide = width // M_CHUNKS
    blocks = wide // cols
    each = part + blocks * rows_dn

    def kernel(m1g, m2g, m1d, m2d, *refs):
        outs, (gu, dn, sems) = refs[:M_CHUNKS], refs[M_CHUNKS:]
        copies = []
        for n in range(M_CHUNKS):
            rows, columns = pl.ds(n * part, part), pl.ds(n * wide, wide)
            copies.append(
                start_all(
                    [
                        (m1g.at[0, rows], gu.at[0, rows]),
                        (m2g.at[0, rows], gu.at[1, rows]),
                        (m1d.at[0, :, columns], dn.at[0, :, columns]),
                        (m2d.at[0, :, columns], dn.at[1, :, columns]),
                    ],
                    sems.at[n],
                )
            )
        for n, out in enumerate(outs):
            wait_all(copies[n])
            for k in range(2):
                base = k * each
                out[base : base + part] = gu[k, n * part : (n + 1) * part].astype(out.dtype)
                for b in range(blocks):
                    at = (n * blocks + b) * cols
                    to = base + part + b * rows_dn
                    out[to : to + rows_dn] = dn[k, :, at : at + cols].astype(out.dtype)

    return pl.pallas_call(
        kernel,
        out_shape=tuple(
            jax.ShapeDtypeStruct((2 * each, cols), jnp.bfloat16) for _ in range(M_CHUNKS)
        ),
        in_specs=[ANY] * 4,
        out_specs=(VMEM,) * M_CHUNKS,
        scratch_shapes=[
            pltpu.VMEM((2, rows_gu, cols), jnp.float32),
            pltpu.VMEM((2, rows_dn, width), jnp.float32),
            pltpu.SemaphoreType.DMA((M_CHUNKS, 4)),
        ],
        compiler_params=grant(8),
        cost_estimate=cost(0, 12 * (m1_gu.size + m1_dn.size)),
        name="pack_moments",
    )(*in_hbm(m1_gu, m2_gu, m1_dn, m2_dn))


def pack_weights(gate_up, down):
    _, rows_gu, cols = gate_up.shape
    _, rows_dn, width = down.shape
    blocks = width // cols
    total = rows_gu + blocks * rows_dn
    size = total // W_CHUNKS

    def kernel(gu_ref, down_ref, *refs):
        outs, (buf, sems) = refs[:W_CHUNKS], refs[W_CHUNKS:]
        pairs = [(down_ref.at[0], buf)]
        for n, out in enumerate(outs):
            low = max(n * size, blocks * rows_dn)
            rows = (n + 1) * size - low
            if rows > 0:
                source = gu_ref.at[0, pl.ds(low - blocks * rows_dn, rows)]
                pairs.append((source, out.at[pl.ds(low - n * size, rows)]))
        copies = start_all(pairs, sems)
        copies[0].wait()
        for b in range(blocks):
            n, to = divmod(b * rows_dn, size)
            outs[n][to : to + rows_dn] = buf[:, b * cols : (b + 1) * cols]
        wait_all(copies[1:])

    return pl.pallas_call(
        kernel,
        out_shape=tuple(jax.ShapeDtypeStruct((size, cols), down.dtype) for _ in range(W_CHUNKS)),
        in_specs=[ANY, ANY],
        out_specs=(VMEM,) * W_CHUNKS,
        scratch_shapes=[
            pltpu.VMEM((rows_dn, width), down.dtype),
            pltpu.SemaphoreType.DMA((W_CHUNKS + 1,)),
        ],
        compiler_params=grant(4),
        cost_estimate=cost(0, 4 * total * cols),
        name="pack_weights",
    )(*in_hbm(gate_up, down))


def partial(count, columns):
    return (
        jax.ShapeDtypeStruct((2 * count, columns), jnp.float32),
        jax.ShapeDtypeStruct((2 * count, columns), jnp.bfloat16),
    )


def forward_gu(tokens, tok_near, gu, gu_mate):
    _, count, width = tokens.shape
    half = width // 2
    rows, cols = gu.shape

    def kernel(tok_r, tokn_r, gu_r, gum_r, out, sent, tok, gub, sems):
        chip, core = chip_and_core()
        mine = pl.ds(pl.multiple_of(chip * half, half), half)
        first = pl.ds(pl.multiple_of(core * rows, rows), rows)
        second = pl.ds(pl.multiple_of((1 - core) * rows, rows), rows)
        pairs = [
            (gu_r, gub.at[first]),
            (gum_r, gub.at[second]),
            (tok_r.at[0, :, mine], tok.at[pl.ds(0, count)]),
            (tokn_r, tok.at[pl.ds(count, count)]),
        ]
        wait_all(start_all(pairs, sems))
        pre = jnp.dot(tok[...], gub[...], preferred_element_type=jnp.float32)
        out[...] = pre
        sent[...] = pre.astype(sent.dtype)

    return pl.pallas_call(
        kernel,
        out_shape=partial(count, cols),
        in_specs=[ANY] * 4,
        out_specs=(VMEM, VMEM),
        scratch_shapes=[
            pltpu.VMEM((2 * count, half), jnp.bfloat16),
            pltpu.VMEM((half, cols), jnp.bfloat16),
            pltpu.SemaphoreType.DMA((4,)),
        ],
        compiler_params=grant(8),
        cost_estimate=cost(4 * count * half * cols, 3 * 1024 * 1024),
        name="forward_gu",
    )(*in_hbm(tokens), tok_near, gu, gu_mate)


def forward_dn(grad_out, up_near, parts):
    _, count, width = grad_out.shape
    half = width // 2
    blocks, rows, cols = parts[0].shape
    units = 4 * rows

    def kernel(up_r, upn_r, mine_r, near_r, mate_r, far_r, out, sent, up, dnb, sems):
        chip, core = chip_and_core()
        mine = pl.ds(pl.multiple_of(chip * half, half), half)
        pairs = [
            (up_r.at[0, :, mine], up.at[pl.ds(0, count)]),
            (upn_r, up.at[pl.ds(count, count)]),
            (mine_r, dnb.at[:, chip, core]),
            (near_r, dnb.at[:, 1 - chip, core]),
            (mate_r, dnb.at[:, chip, 1 - core]),
            (far_r, dnb.at[:, 1 - chip, 1 - core]),
        ]
        wait_all(start_all(pairs, sems))
        dh = jnp.zeros((2 * count, units), jnp.float32)
        for b in range(blocks):
            dh += lax.dot_general(
                up[:, b * cols : (b + 1) * cols],
                dnb[b].reshape(units, cols),
                (((1,), (1,)), ((), ())),
                preferred_element_type=jnp.float32,
            )
        out[...] = dh
        sent[...] = dh.astype(sent.dtype)

    return pl.pallas_call(
        kernel,
        out_shape=partial(count, units),
        in_specs=[ANY] * 6,
        out_specs=(VMEM, VMEM),
        scratch_shapes=[
            pltpu.VMEM((2 * count, half), jnp.bfloat16),
            pltpu.VMEM((blocks, 2, 2, rows, cols), jnp.bfloat16),
            pltpu.SemaphoreType.DMA((6,)),
        ],
        compiler_params=grant(8),
        cost_estimate=cost(4 * count * half * units, 3 * 1024 * 1024),
        name="forward_dn",
    )(*in_hbm(grad_out), up_near, *parts)


def backward(pre, pre_near, dh, dh_near, tokens, tok_near, grad_out, up_near, rows, rows_dn):
    _, count, width = tokens.shape
    half = width // 2
    units = 4 * rows_dn
    cols = 2 * units
    blocks = half // cols

    def kernel(pre_r, pren_r, dh_r, dhn_r, tok_r, tokn_r, up_r, upn_r, g_own, g_mate, d_own, d_mate, tok, tokm, up, res, sems):
        chip, core = chip_and_core()
        mine = pl.ds(pl.multiple_of(chip * half, half), half)
        first = pl.multiple_of(core * rows, rows)
        second = pl.multiple_of((1 - core) * rows, rows)
        here = pl.multiple_of(chip * half, half)
        pairs = [
            (up_r.at[0, :, mine], up.at[pl.ds(0, count)]),
            (upn_r, up.at[pl.ds(count, count)]),
            (tok_r.at[0, :, pl.ds(here + second, rows)], tokm.at[pl.ds(0, count)]),
            (tokn_r.at[:, pl.ds(second, rows)], tokm.at[pl.ds(count, count)]),
            (tok_r.at[0, :, pl.ds(here + first, rows)], tok.at[pl.ds(0, count)]),
            (tokn_r.at[:, pl.ds(first, rows)], tok.at[pl.ds(count, count)]),
        ]
        copies = start_all(pairs, sems)

        def whole(own, near):
            return own[...] + jnp.concatenate([near[count:], near[:count]]).astype(jnp.float32)

        full = whole(pre_r, pren_r) * width ** (-0.5)
        gate = full[:, :units]
        upper = full[:, units:]
        dhidden = whole(dh_r, dhn_r) * units ** (-0.5)
        sigma = jax.nn.sigmoid(gate)
        active = gate * sigma
        hidden = (active * upper).astype(jnp.bfloat16)
        dgate = dhidden * upper * (sigma * (1.0 + gate * (1.0 - sigma)))
        dupper = dhidden * active
        dpre = (jnp.concatenate([dgate, dupper], axis=1) * width ** (-0.5)).astype(jnp.bfloat16)
        over_tokens = (((0,), (0,)), ((), ()))
        wait_all(copies[:2])
        for b in range(blocks):
            res[b] = lax.dot_general(
                hidden, up[:, b * cols : (b + 1) * cols], over_tokens, preferred_element_type=jnp.float32
            ) * units ** (-0.5)
        for b in range(blocks):
            for x in range(2):
                base = x * 2 * rows_dn
                d_own[x, b] = res[b, pl.ds(pl.multiple_of(base + core * rows_dn, rows_dn), rows_dn)]
                d_mate[x, b] = res[
                    b, pl.ds(pl.multiple_of(base + (1 - core) * rows_dn, rows_dn), rows_dn)
                ].astype(d_mate.dtype)
        wait_all(copies[2:4])
        g_mate[...] = lax.dot_general(
            tokm[...], dpre, over_tokens, preferred_element_type=jnp.float32
        ).astype(g_mate.dtype)
        wait_all(copies[4:])
        g_own[...] = lax.dot_general(tok[...], dpre, over_tokens, preferred_element_type=jnp.float32)

    f32, bf16 = jnp.float32, jnp.bfloat16
    dn_shape = (2, blocks, rows_dn, cols)
    return pl.pallas_call(
        kernel,
        out_shape=(
            pltpu.VMEM((rows, cols), f32),
            pltpu.VMEM((rows, cols), bf16),
            pltpu.VMEM(dn_shape, f32),
            pltpu.VMEM(dn_shape, bf16),
        ),
        in_specs=[VMEM] * 4 + [ANY] * 4,
        out_specs=(VMEM,) * 4,
        scratch_shapes=[
            pltpu.VMEM((2 * count, rows), bf16),
            pltpu.VMEM((2 * count, rows), bf16),
            pltpu.VMEM((2 * count, half), bf16),
            pltpu.VMEM((blocks, units, cols), f32),
            pltpu.SemaphoreType.DMA((6,)),
        ],
        compiler_params=grant(16),
        cost_estimate=cost(4 * count * half * (cols + units), 6 * 1024 * 1024),
        name="backward",
    )(pre, pre_near, dh, dh_near, *in_hbm(tokens), tok_near, *in_hbm(grad_out), up_near)


def adamw_part(weight, grad, first, second, rate):
    first_new = beta_one * first + (1.0 - beta_one) * grad
    second_new = beta_two * second + (1.0 - beta_two) * grad * grad
    wide = weight.astype(jnp.float32)
    updated = wide - rate * (first_new / (jnp.sqrt(second_new) + epsilon) + decay * wide)
    return updated.astype(jnp.bfloat16), first_new, second_new


def start_moments(mode, members, own_pairs, came_pairs, sems):
    @pl.when(mode == 0)
    def _():
        for n, pairs in enumerate(own_pairs):
            for k, (a, b) in enumerate(pairs):
                pltpu.make_async_copy(a, b, sems.at[n, k]).start()

    for hop in range(members - 1):

        @pl.when(mode == hop + 1)
        def _():
            for n, pairs in enumerate(came_pairs[hop]):
                for k, (a, b) in enumerate(pairs):
                    pltpu.make_async_copy(a, b, sems.at[n, k]).start()


def wait_moments(mode, n, own_pairs, came_pairs, sems):
    @pl.when(mode == 0)
    def _():
        for k, (a, b) in enumerate(own_pairs[n]):
            pltpu.make_async_copy(a, b, sems.at[n, k]).wait()

    @pl.when(mode != 0)
    def _():
        for k, (a, b) in enumerate(came_pairs[0][n]):
            pltpu.make_async_copy(a, b, sems.at[n, k]).wait()


def update_gu(winner, learning, low, high, m1, m2, held, gu, g_own, g_got, done):
    members = winner.shape[0]
    _, rows, cols = m1.shape
    part = rows // M_CHUNKS
    each = held[0].shape[0] // 2
    count = high - low
    start, size = low * part, (high - low) * part
    f32, bf16 = jnp.float32, jnp.bfloat16
    span = pl.ds(start, size)

    def kernel(winner_ref, rate_ref, m1_r, m2_r, gu_r, go_r, gm_r, *refs):
        came = refs[: len(held)]
        refs = refs[len(held) + len(done) :]
        n_w, n_1, n_2, bgu, bgo, bgm, own, moved, o_w, o_1, o_2, sems, msems, osems = refs
        mode = mode_of(winner_ref, members)
        rate = rate_ref[winner_ref[lax.axis_index("member")]]
        own_pairs = [
            [
                (m1_r.at[0, pl.ds(start + n * part, part)], own.at[0, pl.ds(n * part, part)]),
                (m2_r.at[0, pl.ds(start + n * part, part)], own.at[1, pl.ds(n * part, part)]),
            ]
            for n in range(count)
        ]
        came_pairs = [
            [
                [
                    (came[n + STAGGER * hop].at[pl.ds(0, part)], moved.at[n, 0]),
                    (came[n + STAGGER * hop].at[pl.ds(each, part)], moved.at[n, 1]),
                ]
                for n in range(count)
            ]
            for hop in range(members - 1)
        ]
        copies = start_all([(gu_r.at[span], bgu), (go_r.at[span], bgo), (gm_r.at[span], bgm)], sems)
        start_moments(mode, members, own_pairs, came_pairs, msems)
        wait_all(copies)
        outs = []
        for n in range(count):
            wait_moments(mode, n, own_pairs, came_pairs, msems)
            at = slice(n * part, (n + 1) * part)
            first = jnp.where(mode == 0, own[0, at], moved[n, 0].astype(f32))
            second = jnp.where(mode == 0, own[1, at], moved[n, 1].astype(f32))
            grad = bgo[at] + bgm[at].astype(f32)
            o_w[at], o_1[at], o_2[at] = adamw_part(bgu[at], grad, first, second, rate)
            here, there = pl.ds(n * part, part), pl.ds(start + n * part, part)
            outs += start_all(
                [
                    (o_w.at[here], n_w.at[0, there]),
                    (o_1.at[here], n_1.at[0, there]),
                    (o_2.at[here], n_2.at[0, there]),
                ],
                osems.at[n],
            )
        wait_all(outs)

    return pl.pallas_call(
        kernel,
        out_shape=tuple(jax.ShapeDtypeStruct((1, rows, cols), t) for t in (bf16, f32, f32)),
        in_specs=[SMEM, SMEM] + [ANY] * (5 + len(held) + len(done)),
        out_specs=(ANY,) * 3,
        scratch_shapes=[
            pltpu.VMEM((size, cols), bf16),
            pltpu.VMEM((size, cols), f32),
            pltpu.VMEM((size, cols), bf16),
            pltpu.VMEM((2, size, cols), f32),
            pltpu.VMEM((count, 2, part, cols), bf16),
            pltpu.VMEM((size, cols), bf16),
            pltpu.VMEM((size, cols), f32),
            pltpu.VMEM((size, cols), f32),
            pltpu.SemaphoreType.DMA((3,)),
            pltpu.SemaphoreType.DMA((count, 2)),
            pltpu.SemaphoreType.DMA((count, 3)),
        ],
        input_output_aliases={7 + len(held) + n: n for n in range(len(done))},
        compiler_params=grant(12),
        cost_estimate=cost(0, 22 * size * cols),
        name="update_gu",
    )(winner, learning, *in_hbm(m1, m2), *in_vmem(gu, g_own, g_got, *held), *done)


def update_dn(winner, learning, m1, m2, held, dn, d_own, d_got, d_back):
    members = winner.shape[0]
    _, rows, width = m1.shape
    _, blocks, _, cols = dn.shape
    each = held[0].shape[0] // 2
    per = 2 * blocks // M_CHUNKS
    size = per * rows
    base = each - size
    f32, bf16 = jnp.float32, jnp.bfloat16

    def kernel(winner_ref, rate_ref, m1_r, m2_r, dn_r, do_r, dm_r, gb_r, *refs):
        came = refs[: len(held)]
        n_w, n_1, n_2, bdn, bdo, bdm, bgb, grad, own, moved, o_w, o_1, o_2, sems, msems, osems = refs[len(held) :]
        chip, _ = chip_and_core()
        mode = mode_of(winner_ref, members)
        rate = rate_ref[winner_ref[lax.axis_index("member")]]
        own_pairs = [
            [
                (m1_r.at[0, :, pl.ds(n * per * cols, per * cols)], own.at[0, :, pl.ds(n * per * cols, per * cols)]),
                (m2_r.at[0, :, pl.ds(n * per * cols, per * cols)], own.at[1, :, pl.ds(n * per * cols, per * cols)]),
            ]
            for n in range(M_CHUNKS)
        ]
        came_pairs = [
            [
                [
                    (came[n + STAGGER * hop].at[pl.ds(base, size)], moved.at[n, 0]),
                    (came[n + STAGGER * hop].at[pl.ds(each + base, size)], moved.at[n, 1]),
                ]
                for n in range(M_CHUNKS)
            ]
            for hop in range(members - 1)
        ]
        copies = start_all(
            [
                (dn_r, bdn),
                (do_r.at[chip], bdo),
                (dm_r.at[chip], bdm),
                (gb_r, bgb),
            ],
            sems,
        )
        start_moments(mode, members, own_pairs, came_pairs, msems)
        wait_all(copies)
        grad[chip] = bdo[...] + bdm[...].astype(f32)
        grad[1 - chip] = bgb[...].astype(f32)
        outs = []
        for n in range(M_CHUNKS):
            wait_moments(mode, n, own_pairs, came_pairs, msems)
            for i in range(per):
                at = slice((n * per + i) * cols, (n * per + i + 1) * cols)
                sub = slice(i * rows, (i + 1) * rows)
                first = jnp.where(mode == 0, own[0, :, at], moved[n, 0, sub].astype(f32))
                second = jnp.where(mode == 0, own[1, :, at], moved[n, 1, sub].astype(f32))
                side, b = divmod(n * per + i, blocks)
                o_w[:, at], o_1[:, at], o_2[:, at] = adamw_part(bdn[side, b], grad[side, b], first, second, rate)
            if n % 4 == 3:
                at = pl.ds((n - 3) * per * cols, 4 * per * cols)
                outs += start_all(
                    [
                        (o_w.at[:, at], n_w.at[0, :, at]),
                        (o_1.at[:, at], n_1.at[0, :, at]),
                        (o_2.at[:, at], n_2.at[0, :, at]),
                    ],
                    osems.at[n // 4],
                )
        wait_all(outs)

    half = (blocks, rows, cols)
    return pl.pallas_call(
        kernel,
        out_shape=tuple(jax.ShapeDtypeStruct((1, rows, width), t) for t in (bf16, f32, f32)),
        in_specs=[SMEM, SMEM] + [ANY] * (6 + len(held)),
        out_specs=(ANY,) * 3,
        scratch_shapes=[
            pltpu.VMEM((2,) + half, bf16),
            pltpu.VMEM(half, f32),
            pltpu.VMEM(half, bf16),
            pltpu.VMEM(half, bf16),
            pltpu.VMEM((2,) + half, f32),
            pltpu.VMEM((2, rows, width), f32),
            pltpu.VMEM((M_CHUNKS, 2, size, cols), bf16),
            pltpu.VMEM((rows, width), bf16),
            pltpu.VMEM((rows, width), f32),
            pltpu.VMEM((rows, width), f32),
            pltpu.SemaphoreType.DMA((4,)),
            pltpu.SemaphoreType.DMA((M_CHUNKS, 2)),
            pltpu.SemaphoreType.DMA((M_CHUNKS // 4, 3)),
        ],
        compiler_params=grant(10),
        cost_estimate=cost(0, 26 * rows * width),
        name="update_dn",
    )(winner, learning, *in_hbm(m1, m2), *in_vmem(dn, d_own, d_got, d_back, *held))


def on_device_four(
    tokens,
    grad_out,
    gate_up,
    down,
    mom1_gate_up,
    mom2_gate_up,
    mom1_down,
    mom2_down,
    learning,
    winner,
):
    members = lax.axis_size("member")
    member_index = lax.axis_index("member")
    fsdp_index = lax.axis_index("fsdp")
    chip = fsdp_index // 2
    over_x = [(0, 2), (2, 0), (1, 3), (3, 1)]
    over_core = [(0, 1), (1, 0), (2, 3), (3, 2)]
    ring = [(i, (i + 1) % members) for i in range(members)]
    half = tokens.shape[2] // 2
    _, rows_gu, cols = gate_up.shape
    rows_dn = down.shape[1]
    rows_all = rows_gu + down.size // cols
    w_rows = rows_all // W_CHUNKS

    indices = jnp.arange(members, dtype=winner.dtype)
    is_source = jnp.any((winner == member_index) & (indices != member_index))

    def theirs(x):
        return lax.dynamic_slice_in_dim(x[0], (1 - chip) * half, half, axis=1)

    own = list(pack_weights(gate_up, down))
    got = [lax.ppermute(chunk, "member", ring) for chunk in own[:STAGGER]]
    tok_theirs = theirs(after(tokens, *own))
    tok_near = lax.ppermute(tok_theirs, "fsdp", over_x)
    up_theirs = theirs(after(grad_out, tok_theirs))
    up_near = lax.ppermute(up_theirs, "fsdp", over_x)
    got[0] = after(got[0], up_theirs)

    def rows_from(low, high):
        pieces = []
        for c in range(low // w_rows, (high - 1) // w_rows + 1):
            first, stop = max(low, c * w_rows), min(high, (c + 1) * w_rows)
            pieces.append((c, first - c * w_rows, stop - first, first - low))
        return pieces

    def take(low, high):
        pieces = rows_from(low, high)
        kept = [(own[piece[0]],) + piece[1:] for piece in pieces]
        return assemble(winner, kept, held[:], pieces, (high - low, cols))

    rows_d = down.size // cols
    held = []
    last = STAGGER * (members - 2)
    pre = dh = grads = first_gu = None
    for step in range(STAGGER, CHUNKS + last + STAGGER):
        back = got[step - STAGGER]
        if step < CHUNKS:
            back = jnp.where(is_source, own[step], back)
        held.append(back)
        if step < CHUNKS + last:
            got.append(lax.ppermute(back, "member", ring))
        if step == STAGGER:
            own += pack_moments(after(mom1_gate_up, back), mom2_gate_up, mom1_down, mom2_down)
        ready = len(held) - 1 - last
        if ready == (rows_d - 1) // w_rows:
            dn = take(0, rows_d).reshape(2, -1, rows_dn, cols)
            dn_mine = lax.dynamic_index_in_dim(dn, chip, axis=0, keepdims=False)
            dn_theirs = lax.dynamic_index_in_dim(dn, 1 - chip, axis=0, keepdims=False)
            dn_near = lax.ppermute(dn_theirs, "fsdp", over_x)
            dn_mate = lax.ppermute(dn_mine, "fsdp", over_core)
        if step == FAR_AT:
            dn_near = after(dn_near, back)
            dn_far = lax.ppermute(dn_near, "fsdp", over_core)
        if ready == W_CHUNKS - 1:
            gu = take(rows_d, rows_all)
            gu_mate = lax.ppermute(gu, "fsdp", over_core)
        if step == GU_AT:
            pre, pre_sent = forward_gu(tokens, tok_near, after(gu, back), gu_mate)
            pre_near = lax.ppermute(pre_sent, "fsdp", over_x)
        if step == DN_AT:
            dh, dh_sent = forward_dn(
                grad_out, up_near, (after(dn_mine, back), dn_near, dn_mate, dn_far)
            )
            dh_near = lax.ppermute(dh_sent, "fsdp", over_x)
        if step == BACK_AT:
            g_own, g_mate, d_own, d_mate = backward(
                after(pre, back), pre_near, dh, dh_near, tokens, tok_near, grad_out, up_near, rows_gu, rows_dn
            )
            g_got = lax.ppermute(g_mate, "fsdp", over_core)
            d_got = lax.ppermute(d_mate, "fsdp", over_core)
        if step == SUM_AT:
            d_there = (
                lax.dynamic_index_in_dim(after(d_own, back), 1 - chip, axis=0, keepdims=False)
                + lax.dynamic_index_in_dim(d_got, 1 - chip, axis=0, keepdims=False)
            ).astype(jnp.bfloat16)
            d_back = lax.ppermute(d_there, "fsdp", over_x)
        if step == EARLY_AT:
            first_gu = update_gu(
                winner, learning, 0, EARLY, mom1_gate_up, mom2_gate_up,
                held[W_CHUNKS : W_CHUNKS + EARLY + last], after(gu, back), g_own, g_got, ()
            )

    new_gu, new_first_gu, new_second_gu = update_gu(
        winner, learning, EARLY, M_CHUNKS, mom1_gate_up, mom2_gate_up,
        held[W_CHUNKS + EARLY :], gu, g_own, g_got, first_gu
    )
    new_dn, new_first_dn, new_second_dn = update_dn(
        winner, learning, mom1_down, mom2_down, held[W_CHUNKS:], dn, d_own, d_got, d_back
    )
    return (new_gu, new_dn, new_first_gu, new_second_gu, new_first_dn, new_second_dn)


def solution(mesh):
    small = mesh.shape["member"] == 4 and mesh.shape["fsdp"] == 4
    return jax.shard_map(
        on_device_four if small else on_device_any,
        mesh=mesh,
        in_specs=(
            P(("groups", "member"), "fsdp", None),
            P(("groups", "member"), "fsdp", None),
            P(("groups", "member"), "fsdp", None),
            P(("groups", "member"), "fsdp", None),
            P(("groups", "member"), "fsdp", None),
            P(("groups", "member"), "fsdp", None),
            P(("groups", "member"), "fsdp", None),
            P(("groups", "member"), "fsdp", None),
            P("groups"),
            P("groups"),
        ),
        out_specs=(
            P(("groups", "member"), "fsdp", None),
            P(("groups", "member"), "fsdp", None),
            P(("groups", "member"), "fsdp", None),
            P(("groups", "member"), "fsdp", None),
            P(("groups", "member"), "fsdp", None),
            P(("groups", "member"), "fsdp", None),
        ),
        check_vma=False,
    )
```

```python
import functools

import jax
import jax.numpy as jnp
from jax import lax
from jax.experimental import pallas as pl
from jax.experimental.pallas import tpu as pltpu
from jax.sharding import PartitionSpec as P

beta_one = 0.9
beta_two = 0.95
epsilon = 1e-08
decay = 0.1


def spread(block, axis, source):
    block = jnp.where(lax.axis_index(axis) == source, block, jnp.zeros_like(block))
    return lax.psum(block, axis)


def adamw(weight, grad, first, second, rate):
    first_new = beta_one * first + (1.0 - beta_one) * grad
    second_new = beta_two * second + (1.0 - beta_two) * grad * grad
    wide = weight.astype(jnp.float32)
    updated = wide - rate * (first_new / (jnp.sqrt(second_new) + epsilon) + decay * wide)
    return (updated.astype(jnp.bfloat16), first_new, second_new)


def on_device_any(
    tokens,
    grad_out,
    gate_up,
    down,
    mom1_gate_up,
    mom2_gate_up,
    mom1_down,
    mom2_down,
    learning,
    winner,
):
    members = lax.axis_size("member")
    member_index = lax.axis_index("member")
    rows_in = tokens[0]
    upstream = grad_out[0]
    width = rows_in.shape[1]
    units = gate_up.shape[2] // 2
    shard_gu = gate_up[0]
    shard_dn = down[0]
    cut = shard_gu.size // members

    def joined(first_part, second_part):
        return jnp.concatenate(
            [first_part.reshape(members, -1), second_part.reshape(members, -1)], axis=1
        )

    def parted(flat):
        return (flat[:, :cut].reshape(shard_gu.shape), flat[:, cut:].reshape(shard_dn.shape))

    own_source = winner[member_index]

    def take_root(root, carry):
        sent_gu, sent_dn = (spread(shard_gu, "member", root), spread(shard_dn, "member", root))
        wanted = own_source == root
        return (jnp.where(wanted, sent_gu, carry[0]), jnp.where(wanted, sent_dn, carry[1]))

    copied_gu, copied_dn = lax.fori_loop(0, members, take_root, (shard_gu, shard_dn))
    first_gu, first_dn = parted(
        lax.all_to_all(
            jnp.take(
                lax.all_to_all(
                    joined(mom1_gate_up[0], mom1_down[0]).astype(jnp.bfloat16),
                    "member",
                    split_axis=0,
                    concat_axis=0,
                    tiled=True,
                ).astype(jnp.float32),
                winner,
                axis=0,
            ).astype(jnp.bfloat16),
            "member",
            split_axis=0,
            concat_axis=0,
            tiled=True,
        ).astype(jnp.float32)
    )
    second_gu, second_dn = parted(
        lax.all_to_all(
            jnp.take(
                lax.all_to_all(
                    joined(mom2_gate_up[0], mom2_down[0]).astype(jnp.bfloat16),
                    "member",
                    split_axis=0,
                    concat_axis=0,
                    tiled=True,
                ).astype(jnp.float32),
                winner,
                axis=0,
            ).astype(jnp.bfloat16),
            "member",
            split_axis=0,
            concat_axis=0,
            tiled=True,
        ).astype(jnp.float32)
    )
    rate = learning[winner[member_index]]
    columns = rows_in
    preact = jnp.dot(
        columns,
        lax.all_gather(copied_gu, "fsdp", axis=0, tiled=True),
        preferred_element_type=jnp.float32,
    ) * width ** (-0.5)
    gate = preact[:, :units]
    upper = preact[:, units:]
    sigma = jax.nn.sigmoid(gate)
    active = gate * sigma
    hidden = (active * upper).astype(jnp.bfloat16)
    dhidden = lax.dot_general(
        upstream,
        lax.all_gather(copied_dn, "fsdp", axis=0, tiled=True),
        (((1,), (1,)), ((), ())),
        preferred_element_type=jnp.float32,
    ) * units ** (-0.5)
    dgate = dhidden * upper * (sigma * (1.0 + gate * (1.0 - sigma)))
    dupper = dhidden * active
    dpreact = (jnp.concatenate([dgate, dupper], axis=1) * width ** (-0.5)).astype(jnp.bfloat16)
    columns = rows_in
    grad_gu = lax.psum_scatter(
        lax.dot_general(
            columns, dpreact, (((0,), (0,)), ((), ())), preferred_element_type=jnp.float32
        ).astype(jnp.bfloat16),
        "fsdp",
        scatter_dimension=0,
        tiled=True,
    ).astype(jnp.float32)
    columns = hidden
    product = lax.dot_general(
        columns, upstream, (((0,), (0,)), ((), ())), preferred_element_type=jnp.float32
    )
    grad_dn = lax.psum_scatter(
        (product * units ** (-0.5)).astype(jnp.bfloat16), "fsdp", scatter_dimension=0, tiled=True
    ).astype(jnp.float32)
    new_gu, new_first_gu, new_second_gu = adamw(copied_gu, grad_gu, first_gu, second_gu, rate)
    new_dn, new_first_dn, new_second_dn = adamw(copied_dn, grad_dn, first_dn, second_dn, rate)
    return (
        new_gu[None],
        new_dn[None],
        new_first_gu[None],
        new_second_gu[None],
        new_first_dn[None],
        new_second_dn[None],
    )


ANY = pl.BlockSpec(memory_space=pl.ANY)
SMEM = pl.BlockSpec(memory_space=pltpu.SMEM)
VMEM = pl.BlockSpec(memory_space=pltpu.VMEM)
STAGGER = 2
W_CHUNKS = 4
M_CHUNKS = 8
CHUNKS = W_CHUNKS + M_CHUNKS
EARLY = 5
NEAR_AT = 8
GU_AT = 10
DN_AT = 11
BACK_AT = 14
SUM_AT = 15
EARLY_AT = 15


def grant(mib):
    return pltpu.CompilerParams(vmem_limit_bytes=mib * 1024 * 1024)


def cost(flops, moved):
    return pl.CostEstimate(flops=flops, bytes_accessed=moved, transcendentals=0)


def in_hbm(*arrays):
    return [pltpu.with_memory_space_constraint(array, pltpu.HBM) for array in arrays]


def in_vmem(*arrays):
    return [pltpu.with_memory_space_constraint(array, pltpu.VMEM) for array in arrays]


def after(value, *others):
    return lax.optimization_barrier((value,) + others)[0]


def mode_of(winner_ref, members):
    member = lax.axis_index("member")
    source = 0
    for other in range(members):
        source = jnp.where(winner_ref[other] != other, winner_ref[other], source)
    return jnp.where(
        winner_ref[member] == member, 0, lax.rem(member - source + members, members)
    )


def chip_and_core():
    index = lax.axis_index("fsdp")
    return index // 2, lax.rem(index, 2)


def start_all(pairs, sems):
    copies = [pltpu.make_async_copy(a, b, sems.at[n]) for n, (a, b) in enumerate(pairs)]
    for copy in copies:
        copy.start()
    return copies


def wait_all(copies):
    for copy in copies:
        copy.wait()


def assemble(winner, own, held, pieces, out_shape):
    members = winner.shape[0]
    arrays = [array for array, _, _, _ in own]

    def kernel(winner_ref, *refs):
        own_refs, came = refs[: len(own)], refs[len(own) : len(own) + len(held)]
        out, sems = refs[len(own) + len(held) :]
        mode = mode_of(winner_ref, members)

        def move(refs, places):
            wait_all(
                start_all(
                    [
                        (ref.at[pl.ds(start, rows)], out.at[pl.ds(to, rows)])
                        for ref, (_, start, rows, to) in zip(refs, places)
                    ],
                    sems,
                )
            )

        @pl.when(mode == 0)
        def _():
            move(own_refs, own)

        for hop in range(members - 1):

            @pl.when(mode == hop + 1)
            def _():
                move([came[place + STAGGER * hop] for place, _, _, _ in pieces], pieces)

    return pl.pallas_call(
        kernel,
        out_shape=jax.ShapeDtypeStruct(out_shape, jnp.bfloat16),
        in_specs=[SMEM] + [ANY] * (len(own) + len(held)),
        out_specs=VMEM,
        scratch_shapes=[pltpu.SemaphoreType.DMA((max(len(own), len(pieces)),))],
        compiler_params=grant(4),
        cost_estimate=cost(0, 4 * out_shape[0] * out_shape[1]),
        name="assemble",
    )(winner, *arrays, *held)


def pack_moments(m1_gu, m2_gu, m1_dn, m2_dn):
    _, rows_gu, cols = m1_gu.shape
    _, rows_dn, width = m1_dn.shape
    part = rows_gu // M_CHUNKS
    wide = width // M_CHUNKS
    blocks = wide // cols
    each = part + blocks * rows_dn

    def kernel(m1g, m2g, m1d, m2d, *refs):
        outs, (gu, dn, sems) = refs[:M_CHUNKS], refs[M_CHUNKS:]
        copies = []
        for n in range(M_CHUNKS):
            rows, columns = pl.ds(n * part, part), pl.ds(n * wide, wide)
            copies.append(
                start_all(
                    [
                        (m1g.at[0, rows], gu.at[0, rows]),
                        (m2g.at[0, rows], gu.at[1, rows]),
                        (m1d.at[0, :, columns], dn.at[0, :, columns]),
                        (m2d.at[0, :, columns], dn.at[1, :, columns]),
                    ],
                    sems.at[n],
                )
            )
        for n, out in enumerate(outs):
            wait_all(copies[n])
            for k in range(2):
                base = k * each
                out[base : base + part] = gu[k, n * part : (n + 1) * part].astype(out.dtype)
                for b in range(blocks):
                    at = (n * blocks + b) * cols
                    to = base + part + b * rows_dn
                    out[to : to + rows_dn] = dn[k, :, at : at + cols].astype(out.dtype)

    return pl.pallas_call(
        kernel,
        out_shape=tuple(
            jax.ShapeDtypeStruct((2 * each, cols), jnp.bfloat16) for _ in range(M_CHUNKS)
        ),
        in_specs=[ANY] * 4,
        out_specs=(VMEM,) * M_CHUNKS,
        scratch_shapes=[
            pltpu.VMEM((2, rows_gu, cols), jnp.float32),
            pltpu.VMEM((2, rows_dn, width), jnp.float32),
            pltpu.SemaphoreType.DMA((M_CHUNKS, 4)),
        ],
        compiler_params=grant(8),
        cost_estimate=cost(0, 12 * (m1_gu.size + m1_dn.size)),
        name="pack_moments",
    )(*in_hbm(m1_gu, m2_gu, m1_dn, m2_dn))


def pack_weights(gate_up, down):
    _, rows_gu, cols = gate_up.shape
    _, rows_dn, width = down.shape
    blocks = width // cols
    total = rows_gu + blocks * rows_dn
    size = total // W_CHUNKS

    def kernel(gu_ref, down_ref, *refs):
        outs, (buf, sems) = refs[:W_CHUNKS], refs[W_CHUNKS:]
        pairs = [(down_ref.at[0], buf)]
        for n, out in enumerate(outs):
            low = max(n * size, blocks * rows_dn)
            rows = (n + 1) * size - low
            if rows > 0:
                source = gu_ref.at[0, pl.ds(low - blocks * rows_dn, rows)]
                pairs.append((source, out.at[pl.ds(low - n * size, rows)]))
        copies = start_all(pairs, sems)
        copies[0].wait()
        for b in range(blocks):
            n, to = divmod(b * rows_dn, size)
            outs[n][to : to + rows_dn] = buf[:, b * cols : (b + 1) * cols]
        wait_all(copies[1:])

    return pl.pallas_call(
        kernel,
        out_shape=tuple(jax.ShapeDtypeStruct((size, cols), down.dtype) for _ in range(W_CHUNKS)),
        in_specs=[ANY, ANY],
        out_specs=(VMEM,) * W_CHUNKS,
        scratch_shapes=[
            pltpu.VMEM((rows_dn, width), down.dtype),
            pltpu.SemaphoreType.DMA((W_CHUNKS + 1,)),
        ],
        compiler_params=grant(4),
        cost_estimate=cost(0, 4 * total * cols),
        name="pack_weights",
    )(*in_hbm(gate_up, down))


def partial(count, columns):
    return (
        jax.ShapeDtypeStruct((2 * count, columns), jnp.float32),
        jax.ShapeDtypeStruct((2 * count, columns), jnp.bfloat16),
    )


def forward_gu(tokens, tok_near, gu, gu_mate):
    _, count, width = tokens.shape
    half = width // 2
    rows, cols = gu.shape

    def kernel(tok_r, tokn_r, gu_r, gum_r, out, sent, tok, gub, sems):
        chip, core = chip_and_core()
        mine = pl.ds(pl.multiple_of(chip * half, half), half)
        first = pl.ds(pl.multiple_of(core * rows, rows), rows)
        second = pl.ds(pl.multiple_of((1 - core) * rows, rows), rows)
        pairs = [
            (gu_r, gub.at[first]),
            (gum_r, gub.at[second]),
            (tok_r.at[0, :, mine], tok.at[pl.ds(0, count)]),
            (tokn_r, tok.at[pl.ds(count, count)]),
        ]
        wait_all(start_all(pairs, sems))
        pre = jnp.dot(tok[...], gub[...], preferred_element_type=jnp.float32)
        out[...] = pre
        sent[...] = pre.astype(sent.dtype)

    return pl.pallas_call(
        kernel,
        out_shape=partial(count, cols),
        in_specs=[ANY] * 4,
        out_specs=(VMEM, VMEM),
        scratch_shapes=[
            pltpu.VMEM((2 * count, half), jnp.bfloat16),
            pltpu.VMEM((half, cols), jnp.bfloat16),
            pltpu.SemaphoreType.DMA((4,)),
        ],
        compiler_params=grant(8),
        cost_estimate=cost(4 * count * half * cols, 3 * 1024 * 1024),
        name="forward_gu",
    )(*in_hbm(tokens), tok_near, gu, gu_mate)


def forward_dn(grad_out, up_near, parts):
    _, count, width = grad_out.shape
    half = width // 2
    blocks, rows, cols = parts[0].shape
    units = 4 * rows

    def kernel(up_r, upn_r, mine_r, near_r, mate_r, far_r, out, sent, up, dnb, sems):
        chip, core = chip_and_core()
        mine = pl.ds(pl.multiple_of(chip * half, half), half)
        pairs = [
            (up_r.at[0, :, mine], up.at[pl.ds(0, count)]),
            (upn_r, up.at[pl.ds(count, count)]),
            (mine_r, dnb.at[:, chip, core]),
            (near_r, dnb.at[:, 1 - chip, core]),
            (mate_r, dnb.at[:, chip, 1 - core]),
            (far_r, dnb.at[:, 1 - chip, 1 - core]),
        ]
        wait_all(start_all(pairs, sems))
        dh = jnp.zeros((2 * count, units), jnp.float32)
        for b in range(blocks):
            dh += lax.dot_general(
                up[:, b * cols : (b + 1) * cols],
                dnb[b].reshape(units, cols),
                (((1,), (1,)), ((), ())),
                preferred_element_type=jnp.float32,
            )
        out[...] = dh
        sent[...] = dh.astype(sent.dtype)

    return pl.pallas_call(
        kernel,
        out_shape=partial(count, units),
        in_specs=[ANY] * 6,
        out_specs=(VMEM, VMEM),
        scratch_shapes=[
            pltpu.VMEM((2 * count, half), jnp.bfloat16),
            pltpu.VMEM((blocks, 2, 2, rows, cols), jnp.bfloat16),
            pltpu.SemaphoreType.DMA((6,)),
        ],
        compiler_params=grant(8),
        cost_estimate=cost(4 * count * half * units, 3 * 1024 * 1024),
        name="forward_dn",
    )(*in_hbm(grad_out), up_near, *parts)


def backward(pre, pre_near, dh, dh_near, tokens, tok_near, grad_out, up_near, rows, rows_dn):
    _, count, width = tokens.shape
    half = width // 2
    units = 4 * rows_dn
    cols = 2 * units
    blocks = half // cols

    def kernel(pre_r, pren_r, dh_r, dhn_r, tok_r, tokn_r, up_r, upn_r, g_own, g_mate, d_own, d_mate, tok, tokm, up, res, sems):
        chip, core = chip_and_core()
        mine = pl.ds(pl.multiple_of(chip * half, half), half)
        first = pl.multiple_of(core * rows, rows)
        second = pl.multiple_of((1 - core) * rows, rows)
        here = pl.multiple_of(chip * half, half)
        pairs = [
            (up_r.at[0, :, mine], up.at[pl.ds(0, count)]),
            (upn_r, up.at[pl.ds(count, count)]),
            (tok_r.at[0, :, pl.ds(here + second, rows)], tokm.at[pl.ds(0, count)]),
            (tokn_r.at[:, pl.ds(second, rows)], tokm.at[pl.ds(count, count)]),
            (tok_r.at[0, :, pl.ds(here + first, rows)], tok.at[pl.ds(0, count)]),
            (tokn_r.at[:, pl.ds(first, rows)], tok.at[pl.ds(count, count)]),
        ]
        copies = start_all(pairs, sems)

        def whole(own, near):
            return own[...] + jnp.concatenate([near[count:], near[:count]]).astype(jnp.float32)

        full = whole(pre_r, pren_r) * width ** (-0.5)
        gate = full[:, :units]
        upper = full[:, units:]
        dhidden = whole(dh_r, dhn_r) * units ** (-0.5)
        sigma = jax.nn.sigmoid(gate)
        active = gate * sigma
        hidden = (active * upper).astype(jnp.bfloat16)
        dgate = dhidden * upper * (sigma * (1.0 + gate * (1.0 - sigma)))
        dupper = dhidden * active
        dpre = (jnp.concatenate([dgate, dupper], axis=1) * width ** (-0.5)).astype(jnp.bfloat16)
        over_tokens = (((0,), (0,)), ((), ()))
        wait_all(copies[:2])
        for b in range(blocks):
            res[b] = lax.dot_general(
                hidden, up[:, b * cols : (b + 1) * cols], over_tokens, preferred_element_type=jnp.float32
            ) * units ** (-0.5)
        for b in range(blocks):
            for x in range(2):
                base = x * 2 * rows_dn
                d_own[x, b] = res[b, pl.ds(pl.multiple_of(base + core * rows_dn, rows_dn), rows_dn)]
                d_mate[x, b] = res[
                    b, pl.ds(pl.multiple_of(base + (1 - core) * rows_dn, rows_dn), rows_dn)
                ].astype(d_mate.dtype)
        wait_all(copies[2:4])
        g_mate[...] = lax.dot_general(
            tokm[...], dpre, over_tokens, preferred_element_type=jnp.float32
        ).astype(g_mate.dtype)
        wait_all(copies[4:])
        g_own[...] = lax.dot_general(tok[...], dpre, over_tokens, preferred_element_type=jnp.float32)

    f32, bf16 = jnp.float32, jnp.bfloat16
    dn_shape = (2, blocks, rows_dn, cols)
    return pl.pallas_call(
        kernel,
        out_shape=(
            pltpu.VMEM((rows, cols), f32),
            pltpu.VMEM((rows, cols), bf16),
            pltpu.VMEM(dn_shape, f32),
            pltpu.VMEM(dn_shape, bf16),
        ),
        in_specs=[VMEM] * 4 + [ANY] * 4,
        out_specs=(VMEM,) * 4,
        scratch_shapes=[
            pltpu.VMEM((2 * count, rows), bf16),
            pltpu.VMEM((2 * count, rows), bf16),
            pltpu.VMEM((2 * count, half), bf16),
            pltpu.VMEM((blocks, units, cols), f32),
            pltpu.SemaphoreType.DMA((6,)),
        ],
        compiler_params=grant(16),
        cost_estimate=cost(4 * count * half * (cols + units), 6 * 1024 * 1024),
        name="backward",
    )(pre, pre_near, dh, dh_near, *in_hbm(tokens), tok_near, *in_hbm(grad_out), up_near)


def adamw_part(weight, grad, first, second, rate):
    first_new = beta_one * first + (1.0 - beta_one) * grad
    second_new = beta_two * second + (1.0 - beta_two) * grad * grad
    wide = weight.astype(jnp.float32)
    updated = wide - rate * (first_new / (jnp.sqrt(second_new) + epsilon) + decay * wide)
    return updated.astype(jnp.bfloat16), first_new, second_new


def start_moments(mode, members, own_pairs, came_pairs, sems):
    @pl.when(mode == 0)
    def _():
        for n, pairs in enumerate(own_pairs):
            for k, (a, b) in enumerate(pairs):
                pltpu.make_async_copy(a, b, sems.at[n, k]).start()

    for hop in range(members - 1):

        @pl.when(mode == hop + 1)
        def _():
            for n, pairs in enumerate(came_pairs[hop]):
                for k, (a, b) in enumerate(pairs):
                    pltpu.make_async_copy(a, b, sems.at[n, k]).start()


def wait_moments(mode, n, own_pairs, came_pairs, sems):
    @pl.when(mode == 0)
    def _():
        for k, (a, b) in enumerate(own_pairs[n]):
            pltpu.make_async_copy(a, b, sems.at[n, k]).wait()

    @pl.when(mode != 0)
    def _():
        for k, (a, b) in enumerate(came_pairs[0][n]):
            pltpu.make_async_copy(a, b, sems.at[n, k]).wait()


def gate_up_rows(mode, rate, members, low, high, each, ins, came, outs, scratch):
    m1_r, m2_r, gu_r, go_r, gm_r = ins
    n_w, n_1, n_2 = outs
    bgu, bgo, bgm, own, moved, o_w, o_1, o_2, sems, msems, osems = scratch
    part = m1_r.shape[1] // M_CHUNKS
    start, count = low * part, high - low
    span = pl.ds(start, count * part)
    own_pairs = [
        [
            (m1_r.at[0, pl.ds(start + n * part, part)], own.at[0, pl.ds(n * part, part)]),
            (m2_r.at[0, pl.ds(start + n * part, part)], own.at[1, pl.ds(n * part, part)]),
        ]
        for n in range(count)
    ]
    came_pairs = [
        [
            [
                (came[low + n + STAGGER * hop].at[pl.ds(0, part)], moved.at[n, 0]),
                (came[low + n + STAGGER * hop].at[pl.ds(each, part)], moved.at[n, 1]),
            ]
            for n in range(count)
        ]
        for hop in range(members - 1)
    ]
    copies = start_all([(gu_r.at[span], bgu), (go_r.at[span], bgo), (gm_r.at[span], bgm)], sems)
    start_moments(mode, members, own_pairs, came_pairs, msems)

    def finish():
        wait_all(copies)
        sent = []
        for n in range(count):
            wait_moments(mode, n, own_pairs, came_pairs, msems)
            at = slice(n * part, (n + 1) * part)
            first = jnp.where(mode == 0, own[0, at], moved[n, 0].astype(jnp.float32))
            second = jnp.where(mode == 0, own[1, at], moved[n, 1].astype(jnp.float32))
            grad = bgo[at] + bgm[at].astype(jnp.float32)
            o_w[at], o_1[at], o_2[at] = adamw_part(bgu[at], grad, first, second, rate)
            here, there = pl.ds(n * part, part), pl.ds(start + n * part, part)
            sent += start_all(
                [
                    (o_w.at[here], n_w.at[0, there]),
                    (o_1.at[here], n_1.at[0, there]),
                    (o_2.at[here], n_2.at[0, there]),
                ],
                osems.at[n],
            )
        return sent

    return finish


def down_rows(mode, rate, members, each, ins, came, outs, scratch):
    m1_r, m2_r, dn_r, do_r, dm_r, gb_r = ins
    n_w, n_1, n_2 = outs
    bdn, bdo, bdm, bgb, grad, own, moved, o_w, o_1, o_2, sems, msems, osems = scratch
    _, rows, width = m1_r.shape
    _, blocks, _, cols = dn_r.shape
    per = 2 * blocks // M_CHUNKS
    size = per * rows
    base = each - size
    chip, _ = chip_and_core()
    spans = [pl.ds(n * per * cols, per * cols) for n in range(M_CHUNKS)]
    own_pairs = [
        [(m1_r.at[0, :, span], own.at[0, :, span]), (m2_r.at[0, :, span], own.at[1, :, span])]
        for span in spans
    ]
    came_pairs = [
        [
            [
                (came[n + STAGGER * hop].at[pl.ds(base, size)], moved.at[n, 0]),
                (came[n + STAGGER * hop].at[pl.ds(each + base, size)], moved.at[n, 1]),
            ]
            for n in range(M_CHUNKS)
        ]
        for hop in range(members - 1)
    ]
    copies = start_all([(dn_r, bdn), (do_r.at[chip], bdo), (dm_r.at[chip], bdm), (gb_r, bgb)], sems)
    start_moments(mode, members, own_pairs, came_pairs, msems)

    def finish():
        wait_all(copies)
        grad[chip] = bdo[...] + bdm[...].astype(jnp.float32)
        grad[1 - chip] = bgb[...].astype(jnp.float32)
        sent = []
        for n in range(M_CHUNKS):
            wait_moments(mode, n, own_pairs, came_pairs, msems)
            for i in range(per):
                at = slice((n * per + i) * cols, (n * per + i + 1) * cols)
                sub = slice(i * rows, (i + 1) * rows)
                first = jnp.where(mode == 0, own[0, :, at], moved[n, 0, sub].astype(jnp.float32))
                second = jnp.where(mode == 0, own[1, :, at], moved[n, 1, sub].astype(jnp.float32))
                side, b = divmod(n * per + i, blocks)
                o_w[:, at], o_1[:, at], o_2[:, at] = adamw_part(
                    bdn[side, b], grad[side, b], first, second, rate
                )
            if n % 2 == 1:
                at = pl.ds((n - 1) * per * cols, 2 * per * cols)
                sent += start_all(
                    [
                        (o_w.at[:, at], n_w.at[0, :, at]),
                        (o_1.at[:, at], n_1.at[0, :, at]),
                        (o_2.at[:, at], n_2.at[0, :, at]),
                    ],
                    osems.at[n // 2],
                )
        return sent

    return finish


def update(winner, learning, low, high, held, gate_up_side, done=(), down_side=()):
    members = winner.shape[0]
    m1, m2, gu, g_own, g_got = gate_up_side
    _, rows, cols = m1.shape
    part = rows // M_CHUNKS
    each = held[0].shape[0] // 2
    count = high - low
    size = count * part
    f32, bf16 = jnp.float32, jnp.bfloat16
    scratch = [
        pltpu.VMEM((size, cols), bf16),
        pltpu.VMEM((size, cols), f32),
        pltpu.VMEM((size, cols), bf16),
        pltpu.VMEM((2, size, cols), f32),
        pltpu.VMEM((count, 2, part, cols), bf16),
        pltpu.VMEM((size, cols), bf16),
        pltpu.VMEM((size, cols), f32),
        pltpu.VMEM((size, cols), f32),
        pltpu.SemaphoreType.DMA((3,)),
        pltpu.SemaphoreType.DMA((count, 2)),
        pltpu.SemaphoreType.DMA((count, 3)),
    ]
    shapes = [jax.ShapeDtypeStruct((1, rows, cols), t) for t in (bf16, f32, f32)]
    operands = [*in_hbm(m1, m2), *in_vmem(gu, g_own, g_got)]
    if down_side:
        n1, n2, dn, d_own, d_got, d_back = down_side
        _, rows_dn, width = n1.shape
        half = dn.shape[1:]
        moved = (width // cols // M_CHUNKS) * rows_dn
        scratch += [
            pltpu.VMEM((2,) + half, bf16),
            pltpu.VMEM(half, f32),
            pltpu.VMEM(half, bf16),
            pltpu.VMEM(half, bf16),
            pltpu.VMEM((2,) + half, f32),
            pltpu.VMEM((2, rows_dn, width), f32),
            pltpu.VMEM((M_CHUNKS, 2, moved, cols), bf16),
            pltpu.VMEM((rows_dn, width), bf16),
            pltpu.VMEM((rows_dn, width), f32),
            pltpu.VMEM((rows_dn, width), f32),
            pltpu.SemaphoreType.DMA((4,)),
            pltpu.SemaphoreType.DMA((M_CHUNKS, 2)),
            pltpu.SemaphoreType.DMA((M_CHUNKS // 2, 3)),
        ]
        shapes += [jax.ShapeDtypeStruct((1, rows_dn, width), t) for t in (bf16, f32, f32)]
        operands += [*in_hbm(n1, n2), *in_vmem(dn, d_own, d_got, d_back)]
    fixed = len(operands)

    def kernel(winner_ref, rate_ref, *refs):
        ins, refs = refs[:fixed], refs[fixed:]
        came, refs = refs[: len(held)], refs[len(held) + len(done) :]
        outs, temps = refs[: len(shapes)], refs[len(shapes) :]
        mode = mode_of(winner_ref, members)
        rate = rate_ref[winner_ref[lax.axis_index("member")]]
        finish = [
            gate_up_rows(mode, rate, members, low, high, each, ins[:5], came, outs[:3], temps[:11])
        ]
        if down_side:
            finish.append(down_rows(mode, rate, members, each, ins[5:], came, outs[3:], temps[11:]))
        sent = [copy for part in finish for copy in part()]
        wait_all(sent)

    return pl.pallas_call(
        kernel,
        out_shape=tuple(shapes),
        in_specs=[SMEM, SMEM] + [ANY] * (fixed + len(held) + len(done)),
        out_specs=(ANY,) * len(shapes),
        scratch_shapes=scratch,
        input_output_aliases={2 + fixed + len(held) + n: n for n in range(len(done))},
        compiler_params=grant(16),
        cost_estimate=cost(0, 22 * size * cols),
        name="update",
    )(winner, learning, *operands, *in_vmem(*held), *done)


def on_device_four(
    tokens,
    grad_out,
    gate_up,
    down,
    mom1_gate_up,
    mom2_gate_up,
    mom1_down,
    mom2_down,
    learning,
    winner,
):
    members = lax.axis_size("member")
    member_index = lax.axis_index("member")
    fsdp_index = lax.axis_index("fsdp")
    chip = fsdp_index // 2
    over_x = [(0, 2), (2, 0), (1, 3), (3, 1)]
    over_core = [(0, 1), (1, 0), (2, 3), (3, 2)]
    over_both = [(0, 3), (3, 0), (1, 2), (2, 1)]
    ring = [(i, (i + 1) % members) for i in range(members)]
    half = tokens.shape[2] // 2
    _, rows_gu, cols = gate_up.shape
    rows_dn = down.shape[1]
    rows_all = rows_gu + down.size // cols
    w_rows = rows_all // W_CHUNKS

    indices = jnp.arange(members, dtype=winner.dtype)
    is_source = jnp.any((winner == member_index) & (indices != member_index))

    def theirs(x):
        return lax.dynamic_slice_in_dim(x[0], (1 - chip) * half, half, axis=1)

    own = list(pack_weights(gate_up, down))
    got = [lax.ppermute(chunk, "member", ring) for chunk in own[:STAGGER]]
    tok_theirs = theirs(after(tokens, *own))
    tok_near = lax.ppermute(tok_theirs, "fsdp", over_x)
    up_theirs = theirs(after(grad_out, tok_theirs))
    up_near = lax.ppermute(up_theirs, "fsdp", over_x)

    def rows_from(low, high):
        pieces = []
        for c in range(low // w_rows, (high - 1) // w_rows + 1):
            first, stop = max(low, c * w_rows), min(high, (c + 1) * w_rows)
            pieces.append((c, first - c * w_rows, stop - first, first - low))
        return pieces

    def take(low, high):
        pieces = rows_from(low, high)
        kept = [(own[piece[0]],) + piece[1:] for piece in pieces]
        return assemble(winner, kept, held[:], pieces, (high - low, cols))

    rows_d = down.size // cols
    held = []
    gap = [up_theirs]
    last = STAGGER * (members - 2)
    pre = dh = grads = first_gu = None
    for step in range(STAGGER, CHUNKS + last + STAGGER):
        back = after(got[step - STAGGER], *gap)
        gap = []
        if step < CHUNKS:
            back = jnp.where(is_source, own[step], back)
        held.append(back)
        gap = [back]
        if step < CHUNKS + last:
            got.append(lax.ppermute(back, "member", ring))
        if step == STAGGER:
            own += pack_moments(after(mom1_gate_up, back), mom2_gate_up, mom1_down, mom2_down)
        ready = len(held) - 1 - last
        if ready == (rows_d - 1) // w_rows:
            dn = take(0, rows_d).reshape(2, -1, rows_dn, cols)
            dn_mine = lax.dynamic_index_in_dim(dn, chip, axis=0, keepdims=False)
            dn_theirs = lax.dynamic_index_in_dim(dn, 1 - chip, axis=0, keepdims=False)
            dn_near = lax.ppermute(dn_theirs, "fsdp", over_x)
            dn_mate = lax.ppermute(dn_mine, "fsdp", over_core)
            dn_far = lax.ppermute(dn_theirs, "fsdp", over_both)
        if step == NEAR_AT:
            gap += [dn_near, dn_far, dn_mate]
        if ready == W_CHUNKS - 1:
            gu = take(rows_d, rows_all)
            gu_mate = lax.ppermute(gu, "fsdp", over_core)
        if step == GU_AT:
            pre, pre_sent = forward_gu(tokens, tok_near, after(gu, back), gu_mate)
            pre_near = lax.ppermute(pre_sent, "fsdp", over_x)
        if step == DN_AT:
            dh, dh_sent = forward_dn(
                grad_out, up_near, (after(dn_mine, back), dn_near, dn_mate, dn_far)
            )
            dh_near = lax.ppermute(dh_sent, "fsdp", over_x)
        if step == BACK_AT:
            g_own, g_mate, d_own, d_mate = backward(
                after(pre, back), pre_near, dh, dh_near, tokens, tok_near, grad_out, up_near, rows_gu, rows_dn
            )
            g_got = lax.ppermute(g_mate, "fsdp", over_core)
            d_got = lax.ppermute(d_mate, "fsdp", over_core)
        if step == SUM_AT:
            d_there = (
                lax.dynamic_index_in_dim(after(d_own, back), 1 - chip, axis=0, keepdims=False)
                + lax.dynamic_index_in_dim(d_got, 1 - chip, axis=0, keepdims=False)
            ).astype(jnp.bfloat16)
            d_back = lax.ppermute(d_there, "fsdp", over_x)
        if step == EARLY_AT:
            first_gu = update(
                winner,
                learning,
                0,
                EARLY,
                held[W_CHUNKS : W_CHUNKS + EARLY + last],
                (mom1_gate_up, mom2_gate_up, after(gu, back), g_own, g_got),
            )
            gap = list(first_gu)

    new_gu, new_first_gu, new_second_gu, new_dn, new_first_dn, new_second_dn = update(
        winner,
        learning,
        EARLY,
        M_CHUNKS,
        held[W_CHUNKS:],
        (mom1_gate_up, mom2_gate_up, gu, g_own, g_got),
        first_gu,
        (mom1_down, mom2_down, dn, d_own, d_got, d_back),
    )
    return (new_gu, new_dn, new_first_gu, new_second_gu, new_first_dn, new_second_dn)


def solution(mesh):
    small = mesh.shape["member"] == 4 and mesh.shape["fsdp"] == 4
    return jax.shard_map(
        on_device_four if small else on_device_any,
        mesh=mesh,
        in_specs=(
            P(("groups", "member"), "fsdp", None),
            P(("groups", "member"), "fsdp", None),
            P(("groups", "member"), "fsdp", None),
            P(("groups", "member"), "fsdp", None),
            P(("groups", "member"), "fsdp", None),
            P(("groups", "member"), "fsdp", None),
            P(("groups", "member"), "fsdp", None),
            P(("groups", "member"), "fsdp", None),
            P("groups"),
            P("groups"),
        ),
        out_specs=(
            P(("groups", "member"), "fsdp", None),
            P(("groups", "member"), "fsdp", None),
            P(("groups", "member"), "fsdp", None),
            P(("groups", "member"), "fsdp", None),
            P(("groups", "member"), "fsdp", None),
            P(("groups", "member"), "fsdp", None),
        ),
        check_vma=False,
    )
```

```python
import functools

import jax
import jax.numpy as jnp
from jax import lax
from jax.experimental import pallas as pl
from jax.experimental.pallas import tpu as pltpu
from jax.sharding import PartitionSpec as P

beta_one = 0.9
beta_two = 0.95
epsilon = 1e-08
decay = 0.1


def spread(block, axis, source):
    block = jnp.where(lax.axis_index(axis) == source, block, jnp.zeros_like(block))
    return lax.psum(block, axis)


def adamw(weight, grad, first, second, rate):
    first_new = beta_one * first + (1.0 - beta_one) * grad
    second_new = beta_two * second + (1.0 - beta_two) * grad * grad
    wide = weight.astype(jnp.float32)
    updated = wide - rate * (first_new / (jnp.sqrt(second_new) + epsilon) + decay * wide)
    return (updated.astype(jnp.bfloat16), first_new, second_new)


def on_device_any(
    tokens,
    grad_out,
    gate_up,
    down,
    mom1_gate_up,
    mom2_gate_up,
    mom1_down,
    mom2_down,
    learning,
    winner,
):
    members = lax.axis_size("member")
    member_index = lax.axis_index("member")
    rows_in = tokens[0]
    upstream = grad_out[0]
    width = rows_in.shape[1]
    units = gate_up.shape[2] // 2
    shard_gu = gate_up[0]
    shard_dn = down[0]
    cut = shard_gu.size // members

    def joined(first_part, second_part):
        return jnp.concatenate(
            [first_part.reshape(members, -1), second_part.reshape(members, -1)], axis=1
        )

    def parted(flat):
        return (flat[:, :cut].reshape(shard_gu.shape), flat[:, cut:].reshape(shard_dn.shape))

    own_source = winner[member_index]

    def take_root(root, carry):
        sent_gu, sent_dn = (spread(shard_gu, "member", root), spread(shard_dn, "member", root))
        wanted = own_source == root
        return (jnp.where(wanted, sent_gu, carry[0]), jnp.where(wanted, sent_dn, carry[1]))

    copied_gu, copied_dn = lax.fori_loop(0, members, take_root, (shard_gu, shard_dn))
    first_gu, first_dn = parted(
        lax.all_to_all(
            jnp.take(
                lax.all_to_all(
                    joined(mom1_gate_up[0], mom1_down[0]).astype(jnp.bfloat16),
                    "member",
                    split_axis=0,
                    concat_axis=0,
                    tiled=True,
                ).astype(jnp.float32),
                winner,
                axis=0,
            ).astype(jnp.bfloat16),
            "member",
            split_axis=0,
            concat_axis=0,
            tiled=True,
        ).astype(jnp.float32)
    )
    second_gu, second_dn = parted(
        lax.all_to_all(
            jnp.take(
                lax.all_to_all(
                    joined(mom2_gate_up[0], mom2_down[0]).astype(jnp.bfloat16),
                    "member",
                    split_axis=0,
                    concat_axis=0,
                    tiled=True,
                ).astype(jnp.float32),
                winner,
                axis=0,
            ).astype(jnp.bfloat16),
            "member",
            split_axis=0,
            concat_axis=0,
            tiled=True,
        ).astype(jnp.float32)
    )
    rate = learning[winner[member_index]]
    columns = rows_in
    preact = jnp.dot(
        columns,
        lax.all_gather(copied_gu, "fsdp", axis=0, tiled=True),
        preferred_element_type=jnp.float32,
    ) * width ** (-0.5)
    gate = preact[:, :units]
    upper = preact[:, units:]
    sigma = jax.nn.sigmoid(gate)
    active = gate * sigma
    hidden = (active * upper).astype(jnp.bfloat16)
    dhidden = lax.dot_general(
        upstream,
        lax.all_gather(copied_dn, "fsdp", axis=0, tiled=True),
        (((1,), (1,)), ((), ())),
        preferred_element_type=jnp.float32,
    ) * units ** (-0.5)
    dgate = dhidden * upper * (sigma * (1.0 + gate * (1.0 - sigma)))
    dupper = dhidden * active
    dpreact = (jnp.concatenate([dgate, dupper], axis=1) * width ** (-0.5)).astype(jnp.bfloat16)
    columns = rows_in
    grad_gu = lax.psum_scatter(
        lax.dot_general(
            columns, dpreact, (((0,), (0,)), ((), ())), preferred_element_type=jnp.float32
        ).astype(jnp.bfloat16),
        "fsdp",
        scatter_dimension=0,
        tiled=True,
    ).astype(jnp.float32)
    columns = hidden
    product = lax.dot_general(
        columns, upstream, (((0,), (0,)), ((), ())), preferred_element_type=jnp.float32
    )
    grad_dn = lax.psum_scatter(
        (product * units ** (-0.5)).astype(jnp.bfloat16), "fsdp", scatter_dimension=0, tiled=True
    ).astype(jnp.float32)
    new_gu, new_first_gu, new_second_gu = adamw(copied_gu, grad_gu, first_gu, second_gu, rate)
    new_dn, new_first_dn, new_second_dn = adamw(copied_dn, grad_dn, first_dn, second_dn, rate)
    return (
        new_gu[None],
        new_dn[None],
        new_first_gu[None],
        new_second_gu[None],
        new_first_dn[None],
        new_second_dn[None],
    )


ANY = pl.BlockSpec(memory_space=pl.ANY)
SMEM = pl.BlockSpec(memory_space=pltpu.SMEM)
VMEM = pl.BlockSpec(memory_space=pltpu.VMEM)
STAGGER = 2
W_CHUNKS = 4
M_CHUNKS = 8
CHUNKS = W_CHUNKS + M_CHUNKS
EARLY = 6
NEAR_AT = 8
SEND_AT = 14
GU_AT = 10
DN_AT = 11
BACK_AT = 13
SUM_AT = 15
EARLY_AT = 16


def grant(mib):
    return pltpu.CompilerParams(vmem_limit_bytes=mib * 1024 * 1024)


def cost(flops, moved):
    return pl.CostEstimate(flops=flops, bytes_accessed=moved, transcendentals=0)


def in_hbm(*arrays):
    return [pltpu.with_memory_space_constraint(array, pltpu.HBM) for array in arrays]


def in_vmem(*arrays):
    return [pltpu.with_memory_space_constraint(array, pltpu.VMEM) for array in arrays]


def after(value, *others):
    return lax.optimization_barrier((value,) + others)[0]


def mode_of(winner_ref, members):
    member = lax.axis_index("member")
    source = 0
    for other in range(members):
        source = jnp.where(winner_ref[other] != other, winner_ref[other], source)
    return jnp.where(
        winner_ref[member] == member, 0, lax.rem(member - source + members, members)
    )


def chip_and_core():
    index = lax.axis_index("fsdp")
    return index // 2, lax.rem(index, 2)


def start_all(pairs, sems):
    copies = [pltpu.make_async_copy(a, b, sems.at[n]) for n, (a, b) in enumerate(pairs)]
    for copy in copies:
        copy.start()
    return copies


def wait_all(copies):
    for copy in copies:
        copy.wait()


def assemble(winner, own, held, pieces, out_shape):
    members = winner.shape[0]
    arrays = [array for array, _, _, _ in own]

    def kernel(winner_ref, *refs):
        own_refs, came = refs[: len(own)], refs[len(own) : len(own) + len(held)]
        out, sems = refs[len(own) + len(held) :]
        mode = mode_of(winner_ref, members)

        def move(refs, places):
            wait_all(
                start_all(
                    [
                        (ref.at[pl.ds(start, rows)], out.at[pl.ds(to, rows)])
                        for ref, (_, start, rows, to) in zip(refs, places)
                    ],
                    sems,
                )
            )

        @pl.when(mode == 0)
        def _():
            move(own_refs, own)

        for hop in range(members - 1):

            @pl.when(mode == hop + 1)
            def _():
                move([came[place + STAGGER * hop] for place, _, _, _ in pieces], pieces)

    return pl.pallas_call(
        kernel,
        out_shape=jax.ShapeDtypeStruct(out_shape, jnp.bfloat16),
        in_specs=[SMEM] + [ANY] * (len(own) + len(held)),
        out_specs=VMEM,
        scratch_shapes=[pltpu.SemaphoreType.DMA((max(len(own), len(pieces)),))],
        compiler_params=grant(4),
        cost_estimate=cost(0, 4 * out_shape[0] * out_shape[1]),
        name="assemble",
    )(winner, *arrays, *held)


def pack_moments(m1_gu, m2_gu, m1_dn, m2_dn):
    _, rows_gu, cols = m1_gu.shape
    _, rows_dn, width = m1_dn.shape
    part = rows_gu // M_CHUNKS
    wide = width // M_CHUNKS
    blocks = wide // cols
    each = part + blocks * rows_dn

    def kernel(m1g, m2g, m1d, m2d, *refs):
        outs, (gu, dn, sems) = refs[:M_CHUNKS], refs[M_CHUNKS:]
        copies = []
        for n in range(M_CHUNKS):
            rows, columns = pl.ds(n * part, part), pl.ds(n * wide, wide)
            copies.append(
                start_all(
                    [
                        (m1g.at[0, rows], gu.at[0, rows]),
                        (m2g.at[0, rows], gu.at[1, rows]),
                        (m1d.at[0, :, columns], dn.at[0, :, columns]),
                        (m2d.at[0, :, columns], dn.at[1, :, columns]),
                    ],
                    sems.at[n],
                )
            )
        for n, out in enumerate(outs):
            wait_all(copies[n])
            for k in range(2):
                base = k * each
                out[base : base + part] = gu[k, n * part : (n + 1) * part].astype(out.dtype)
                for b in range(blocks):
                    at = (n * blocks + b) * cols
                    to = base + part + b * rows_dn
                    out[to : to + rows_dn] = dn[k, :, at : at + cols].astype(out.dtype)

    return pl.pallas_call(
        kernel,
        out_shape=tuple(
            jax.ShapeDtypeStruct((2 * each, cols), jnp.bfloat16) for _ in range(M_CHUNKS)
        ),
        in_specs=[ANY] * 4,
        out_specs=(VMEM,) * M_CHUNKS,
        scratch_shapes=[
            pltpu.VMEM((2, rows_gu, cols), jnp.float32),
            pltpu.VMEM((2, rows_dn, width), jnp.float32),
            pltpu.SemaphoreType.DMA((M_CHUNKS, 4)),
        ],
        compiler_params=grant(8),
        cost_estimate=cost(0, 12 * (m1_gu.size + m1_dn.size)),
        name="pack_moments",
    )(*in_hbm(m1_gu, m2_gu, m1_dn, m2_dn))


def pack_weights(gate_up, down):
    _, rows_gu, cols = gate_up.shape
    _, rows_dn, width = down.shape
    blocks = width // cols
    total = rows_gu + blocks * rows_dn
    size = total // W_CHUNKS

    def kernel(gu_ref, down_ref, *refs):
        outs, (buf, sems) = refs[:W_CHUNKS], refs[W_CHUNKS:]
        pairs = [(down_ref.at[0], buf)]
        for n, out in enumerate(outs):
            low = max(n * size, blocks * rows_dn)
            rows = (n + 1) * size - low
            if rows > 0:
                source = gu_ref.at[0, pl.ds(low - blocks * rows_dn, rows)]
                pairs.append((source, out.at[pl.ds(low - n * size, rows)]))
        copies = start_all(pairs, sems)
        copies[0].wait()
        for b in range(blocks):
            n, to = divmod(b * rows_dn, size)
            outs[n][to : to + rows_dn] = buf[:, b * cols : (b + 1) * cols]
        wait_all(copies[1:])

    return pl.pallas_call(
        kernel,
        out_shape=tuple(jax.ShapeDtypeStruct((size, cols), down.dtype) for _ in range(W_CHUNKS)),
        in_specs=[ANY, ANY],
        out_specs=(VMEM,) * W_CHUNKS,
        scratch_shapes=[
            pltpu.VMEM((rows_dn, width), down.dtype),
            pltpu.SemaphoreType.DMA((W_CHUNKS + 1,)),
        ],
        compiler_params=grant(4),
        cost_estimate=cost(0, 4 * total * cols),
        name="pack_weights",
    )(*in_hbm(gate_up, down))


def partial(count, columns):
    return (
        jax.ShapeDtypeStruct((2 * count, columns), jnp.float32),
        jax.ShapeDtypeStruct((2 * count, columns), jnp.bfloat16),
    )


def forward_gu(tokens, tok_near, gu, gu_mate):
    _, count, width = tokens.shape
    half = width // 2
    rows, cols = gu.shape

    def kernel(tok_r, tokn_r, gu_r, gum_r, out, sent, tok, gub, sems):
        chip, core = chip_and_core()
        mine = pl.ds(pl.multiple_of(chip * half, half), half)
        first = pl.ds(pl.multiple_of(core * rows, rows), rows)
        second = pl.ds(pl.multiple_of((1 - core) * rows, rows), rows)
        pairs = [
            (gu_r, gub.at[first]),
            (gum_r, gub.at[second]),
            (tok_r.at[0, :, mine], tok.at[pl.ds(0, count)]),
            (tokn_r, tok.at[pl.ds(count, count)]),
        ]
        wait_all(start_all(pairs, sems))
        pre = jnp.dot(tok[...], gub[...], preferred_element_type=jnp.float32)
        out[...] = pre
        sent[...] = pre.astype(sent.dtype)

    return pl.pallas_call(
        kernel,
        out_shape=partial(count, cols),
        in_specs=[ANY] * 4,
        out_specs=(VMEM, VMEM),
        scratch_shapes=[
            pltpu.VMEM((2 * count, half), jnp.bfloat16),
            pltpu.VMEM((half, cols), jnp.bfloat16),
            pltpu.SemaphoreType.DMA((4,)),
        ],
        compiler_params=grant(8),
        cost_estimate=cost(4 * count * half * cols, 3 * 1024 * 1024),
        name="forward_gu",
    )(*in_hbm(tokens), tok_near, gu, gu_mate)


def forward_dn(grad_out, up_near, parts):
    _, count, width = grad_out.shape
    half = width // 2
    blocks, rows, cols = parts[0].shape
    units = 4 * rows

    def kernel(up_r, upn_r, mine_r, near_r, mate_r, far_r, out, sent, up, dnb, sems):
        chip, core = chip_and_core()
        mine = pl.ds(pl.multiple_of(chip * half, half), half)
        pairs = [
            (up_r.at[0, :, mine], up.at[pl.ds(0, count)]),
            (upn_r, up.at[pl.ds(count, count)]),
            (mine_r, dnb.at[:, chip, core]),
            (near_r, dnb.at[:, 1 - chip, core]),
            (mate_r, dnb.at[:, chip, 1 - core]),
            (far_r, dnb.at[:, 1 - chip, 1 - core]),
        ]
        wait_all(start_all(pairs, sems))
        dh = jnp.zeros((2 * count, units), jnp.float32)
        for b in range(blocks):
            dh += lax.dot_general(
                up[:, b * cols : (b + 1) * cols],
                dnb[b].reshape(units, cols),
                (((1,), (1,)), ((), ())),
                preferred_element_type=jnp.float32,
            )
        out[...] = dh
        sent[...] = dh.astype(sent.dtype)

    return pl.pallas_call(
        kernel,
        out_shape=partial(count, units),
        in_specs=[ANY] * 6,
        out_specs=(VMEM, VMEM),
        scratch_shapes=[
            pltpu.VMEM((2 * count, half), jnp.bfloat16),
            pltpu.VMEM((blocks, 2, 2, rows, cols), jnp.bfloat16),
            pltpu.SemaphoreType.DMA((6,)),
        ],
        compiler_params=grant(8),
        cost_estimate=cost(4 * count * half * units, 3 * 1024 * 1024),
        name="forward_dn",
    )(*in_hbm(grad_out), up_near, *parts)


def backward(pre, pre_near, dh, dh_near, tokens, tok_near, grad_out, up_near, rows, rows_dn):
    _, count, width = tokens.shape
    half = width // 2
    units = 4 * rows_dn
    cols = 2 * units
    blocks = half // cols

    def kernel(pre_r, pren_r, dh_r, dhn_r, tok_r, tokn_r, up_r, upn_r, g_own, g_mate, d_own, d_mate, tok, tokm, up, res, sems):
        chip, core = chip_and_core()
        mine = pl.ds(pl.multiple_of(chip * half, half), half)
        first = pl.multiple_of(core * rows, rows)
        second = pl.multiple_of((1 - core) * rows, rows)
        here = pl.multiple_of(chip * half, half)
        pairs = [
            (up_r.at[0, :, mine], up.at[pl.ds(0, count)]),
            (upn_r, up.at[pl.ds(count, count)]),
            (tok_r.at[0, :, pl.ds(here + second, rows)], tokm.at[pl.ds(0, count)]),
            (tokn_r.at[:, pl.ds(second, rows)], tokm.at[pl.ds(count, count)]),
            (tok_r.at[0, :, pl.ds(here + first, rows)], tok.at[pl.ds(0, count)]),
            (tokn_r.at[:, pl.ds(first, rows)], tok.at[pl.ds(count, count)]),
        ]
        copies = start_all(pairs, sems)

        def whole(own, near):
            return own[...] + jnp.concatenate([near[count:], near[:count]]).astype(jnp.float32)

        full = whole(pre_r, pren_r) * width ** (-0.5)
        gate = full[:, :units]
        upper = full[:, units:]
        dhidden = whole(dh_r, dhn_r) * units ** (-0.5)
        sigma = jax.nn.sigmoid(gate)
        active = gate * sigma
        hidden = (active * upper).astype(jnp.bfloat16)
        dgate = dhidden * upper * (sigma * (1.0 + gate * (1.0 - sigma)))
        dupper = dhidden * active
        dpre = (jnp.concatenate([dgate, dupper], axis=1) * width ** (-0.5)).astype(jnp.bfloat16)
        over_tokens = (((0,), (0,)), ((), ()))
        wait_all(copies[:2])
        for b in range(blocks):
            res[b] = lax.dot_general(
                hidden, up[:, b * cols : (b + 1) * cols], over_tokens, preferred_element_type=jnp.float32
            ) * units ** (-0.5)
        for b in range(blocks):
            for x in range(2):
                base = x * 2 * rows_dn
                d_own[x, b] = res[b, pl.ds(pl.multiple_of(base + core * rows_dn, rows_dn), rows_dn)]
                d_mate[x, b] = res[
                    b, pl.ds(pl.multiple_of(base + (1 - core) * rows_dn, rows_dn), rows_dn)
                ].astype(d_mate.dtype)
        wait_all(copies[2:4])
        g_mate[...] = lax.dot_general(
            tokm[...], dpre, over_tokens, preferred_element_type=jnp.float32
        ).astype(g_mate.dtype)
        wait_all(copies[4:])
        g_own[...] = lax.dot_general(tok[...], dpre, over_tokens, preferred_element_type=jnp.float32)

    f32, bf16 = jnp.float32, jnp.bfloat16
    dn_shape = (2, blocks, rows_dn, cols)
    return pl.pallas_call(
        kernel,
        out_shape=(
            pltpu.VMEM((rows, cols), f32),
            pltpu.VMEM((rows, cols), bf16),
            pltpu.VMEM(dn_shape, f32),
            pltpu.VMEM(dn_shape, bf16),
        ),
        in_specs=[VMEM] * 4 + [ANY] * 4,
        out_specs=(VMEM,) * 4,
        scratch_shapes=[
            pltpu.VMEM((2 * count, rows), bf16),
            pltpu.VMEM((2 * count, rows), bf16),
            pltpu.VMEM((2 * count, half), bf16),
            pltpu.VMEM((blocks, units, cols), f32),
            pltpu.SemaphoreType.DMA((6,)),
        ],
        compiler_params=grant(16),
        cost_estimate=cost(4 * count * half * (cols + units), 6 * 1024 * 1024),
        name="backward",
    )(pre, pre_near, dh, dh_near, *in_hbm(tokens), tok_near, *in_hbm(grad_out), up_near)


def adamw_part(weight, grad, first, second, rate):
    first_new = beta_one * first + (1.0 - beta_one) * grad
    second_new = beta_two * second + (1.0 - beta_two) * grad * grad
    wide = weight.astype(jnp.float32)
    updated = wide - rate * (first_new / (jnp.sqrt(second_new) + epsilon) + decay * wide)
    return updated.astype(jnp.bfloat16), first_new, second_new


def start_moments(mode, members, own_pairs, came_pairs, sems):
    @pl.when(mode == 0)
    def _():
        for n, pairs in enumerate(own_pairs):
            for k, (a, b) in enumerate(pairs):
                pltpu.make_async_copy(a, b, sems.at[n, k]).start()

    for hop in range(members - 1):

        @pl.when(mode == hop + 1)
        def _():
            for n, pairs in enumerate(came_pairs[hop]):
                for k, (a, b) in enumerate(pairs):
                    pltpu.make_async_copy(a, b, sems.at[n, k]).start()


def wait_moments(mode, n, own_pairs, came_pairs, sems):
    @pl.when(mode == 0)
    def _():
        for k, (a, b) in enumerate(own_pairs[n]):
            pltpu.make_async_copy(a, b, sems.at[n, k]).wait()

    @pl.when(mode != 0)
    def _():
        for k, (a, b) in enumerate(came_pairs[0][n]):
            pltpu.make_async_copy(a, b, sems.at[n, k]).wait()


def gate_up_rows(mode, rate, members, low, high, each, ins, came, outs, scratch):
    m1_r, m2_r, gu_r, go_r, gm_r = ins
    n_w, n_1, n_2 = outs
    bgu, bgo, bgm, own, moved, o_w, o_1, o_2, sems, msems, osems = scratch
    part = m1_r.shape[1] // M_CHUNKS
    start, count = low * part, high - low
    span = pl.ds(start, count * part)
    own_pairs = [
        [
            (m1_r.at[0, pl.ds(start + n * part, part)], own.at[0, pl.ds(n * part, part)]),
            (m2_r.at[0, pl.ds(start + n * part, part)], own.at[1, pl.ds(n * part, part)]),
        ]
        for n in range(count)
    ]
    came_pairs = [
        [
            [
                (came[low + n + STAGGER * hop].at[pl.ds(0, part)], moved.at[n, 0]),
                (came[low + n + STAGGER * hop].at[pl.ds(each, part)], moved.at[n, 1]),
            ]
            for n in range(count)
        ]
        for hop in range(members - 1)
    ]
    copies = start_all([(gu_r.at[span], bgu), (go_r.at[span], bgo), (gm_r.at[span], bgm)], sems)
    start_moments(mode, members, own_pairs, came_pairs, msems)

    def finish():
        wait_all(copies)
        sent = []
        for n in range(count):
            wait_moments(mode, n, own_pairs, came_pairs, msems)
            at = slice(n * part, (n + 1) * part)
            first = jnp.where(mode == 0, own[0, at], moved[n, 0].astype(jnp.float32))
            second = jnp.where(mode == 0, own[1, at], moved[n, 1].astype(jnp.float32))
            grad = bgo[at] + bgm[at].astype(jnp.float32)
            o_w[at], o_1[at], o_2[at] = adamw_part(bgu[at], grad, first, second, rate)
            here, there = pl.ds(n * part, part), pl.ds(start + n * part, part)
            sent += start_all(
                [
                    (o_w.at[here], n_w.at[0, there]),
                    (o_1.at[here], n_1.at[0, there]),
                    (o_2.at[here], n_2.at[0, there]),
                ],
                osems.at[n],
            )
        return sent

    return finish


def down_rows(mode, rate, members, each, ins, came, outs, scratch):
    m1_r, m2_r, dn_r, do_r, dm_r, gb_r = ins
    n_w, n_1, n_2 = outs
    bdn, bdo, bdm, bgb, grad, own, moved, o_w, o_1, o_2, sems, msems, osems = scratch
    _, rows, width = m1_r.shape
    _, blocks, _, cols = dn_r.shape
    per = 2 * blocks // M_CHUNKS
    size = per * rows
    base = each - size
    chip, _ = chip_and_core()
    spans = [pl.ds(n * per * cols, per * cols) for n in range(M_CHUNKS)]
    own_pairs = [
        [(m1_r.at[0, :, span], own.at[0, :, span]), (m2_r.at[0, :, span], own.at[1, :, span])]
        for span in spans
    ]
    came_pairs = [
        [
            [
                (came[n + STAGGER * hop].at[pl.ds(base, size)], moved.at[n, 0]),
                (came[n + STAGGER * hop].at[pl.ds(each + base, size)], moved.at[n, 1]),
            ]
            for n in range(M_CHUNKS)
        ]
        for hop in range(members - 1)
    ]
    copies = start_all([(dn_r, bdn), (do_r.at[chip], bdo), (dm_r.at[chip], bdm), (gb_r, bgb)], sems)
    start_moments(mode, members, own_pairs, came_pairs, msems)

    def finish():
        wait_all(copies)
        grad[chip] = bdo[...] + bdm[...].astype(jnp.float32)
        grad[1 - chip] = bgb[...].astype(jnp.float32)
        sent = []
        for n in range(M_CHUNKS):
            wait_moments(mode, n, own_pairs, came_pairs, msems)
            for i in range(per):
                at = slice((n * per + i) * cols, (n * per + i + 1) * cols)
                sub = slice(i * rows, (i + 1) * rows)
                first = jnp.where(mode == 0, own[0, :, at], moved[n, 0, sub].astype(jnp.float32))
                second = jnp.where(mode == 0, own[1, :, at], moved[n, 1, sub].astype(jnp.float32))
                side, b = divmod(n * per + i, blocks)
                o_w[:, at], o_1[:, at], o_2[:, at] = adamw_part(
                    bdn[side, b], grad[side, b], first, second, rate
                )
            if n % 2 == 1:
                at = pl.ds((n - 1) * per * cols, 2 * per * cols)
                sent += start_all(
                    [
                        (o_w.at[:, at], n_w.at[0, :, at]),
                        (o_1.at[:, at], n_1.at[0, :, at]),
                        (o_2.at[:, at], n_2.at[0, :, at]),
                    ],
                    osems.at[n // 2],
                )
        return sent

    return finish


def update(winner, learning, low, high, held, gate_up_side, done=(), down_side=()):
    members = winner.shape[0]
    m1, m2, gu, g_own, g_got = gate_up_side
    _, rows, cols = m1.shape
    part = rows // M_CHUNKS
    each = held[0].shape[0] // 2
    count = high - low
    size = count * part
    f32, bf16 = jnp.float32, jnp.bfloat16
    scratch = [
        pltpu.VMEM((size, cols), bf16),
        pltpu.VMEM((size, cols), f32),
        pltpu.VMEM((size, cols), bf16),
        pltpu.VMEM((2, size, cols), f32),
        pltpu.VMEM((count, 2, part, cols), bf16),
        pltpu.VMEM((size, cols), bf16),
        pltpu.VMEM((size, cols), f32),
        pltpu.VMEM((size, cols), f32),
        pltpu.SemaphoreType.DMA((3,)),
        pltpu.SemaphoreType.DMA((count, 2)),
        pltpu.SemaphoreType.DMA((count, 3)),
    ]
    shapes = [jax.ShapeDtypeStruct((1, rows, cols), t) for t in (bf16, f32, f32)]
    operands = [*in_hbm(m1, m2), *in_vmem(gu, g_own, g_got)]
    if down_side:
        n1, n2, dn, d_own, d_got, d_back = down_side
        _, rows_dn, width = n1.shape
        half = dn.shape[1:]
        moved = (width // cols // M_CHUNKS) * rows_dn
        scratch += [
            pltpu.VMEM((2,) + half, bf16),
            pltpu.VMEM(half, f32),
            pltpu.VMEM(half, bf16),
            pltpu.VMEM(half, bf16),
            pltpu.VMEM((2,) + half, f32),
            pltpu.VMEM((2, rows_dn, width), f32),
            pltpu.VMEM((M_CHUNKS, 2, moved, cols), bf16),
            pltpu.VMEM((rows_dn, width), bf16),
            pltpu.VMEM((rows_dn, width), f32),
            pltpu.VMEM((rows_dn, width), f32),
            pltpu.SemaphoreType.DMA((4,)),
            pltpu.SemaphoreType.DMA((M_CHUNKS, 2)),
            pltpu.SemaphoreType.DMA((M_CHUNKS // 2, 3)),
        ]
        shapes += [jax.ShapeDtypeStruct((1, rows_dn, width), t) for t in (bf16, f32, f32)]
        operands += [*in_hbm(n1, n2), *in_vmem(dn, d_own, d_got, d_back)]
    fixed = len(operands)

    def kernel(winner_ref, rate_ref, *refs):
        ins, refs = refs[:fixed], refs[fixed:]
        came, refs = refs[: len(held)], refs[len(held) + len(done) :]
        outs, temps = refs[: len(shapes)], refs[len(shapes) :]
        mode = mode_of(winner_ref, members)
        rate = rate_ref[winner_ref[lax.axis_index("member")]]
        finish = [
            gate_up_rows(mode, rate, members, low, high, each, ins[:5], came, outs[:3], temps[:11])
        ]
        if down_side:
            finish.append(down_rows(mode, rate, members, each, ins[5:], came, outs[3:], temps[11:]))
        sent = [copy for part in finish for copy in part()]
        wait_all(sent)

    return pl.pallas_call(
        kernel,
        out_shape=tuple(shapes),
        in_specs=[SMEM, SMEM] + [ANY] * (fixed + len(held) + len(done)),
        out_specs=(ANY,) * len(shapes),
        scratch_shapes=scratch,
        input_output_aliases={2 + fixed + len(held) + n: n for n in range(len(done))},
        compiler_params=grant(16),
        cost_estimate=cost(0, 22 * size * cols),
        name="update",
    )(winner, learning, *operands, *in_vmem(*held), *done)


def on_device_four(
    tokens,
    grad_out,
    gate_up,
    down,
    mom1_gate_up,
    mom2_gate_up,
    mom1_down,
    mom2_down,
    learning,
    winner,
):
    members = lax.axis_size("member")
    member_index = lax.axis_index("member")
    fsdp_index = lax.axis_index("fsdp")
    chip = fsdp_index // 2
    over_x = [(0, 2), (2, 0), (1, 3), (3, 1)]
    over_core = [(0, 1), (1, 0), (2, 3), (3, 2)]
    over_both = [(0, 3), (3, 0), (1, 2), (2, 1)]
    ring = [(i, (i + 1) % members) for i in range(members)]
    half = tokens.shape[2] // 2
    _, rows_gu, cols = gate_up.shape
    rows_dn = down.shape[1]
    rows_all = rows_gu + down.size // cols
    w_rows = rows_all // W_CHUNKS

    indices = jnp.arange(members, dtype=winner.dtype)
    is_source = jnp.any((winner == member_index) & (indices != member_index))

    def theirs(x):
        return lax.dynamic_slice_in_dim(x[0], (1 - chip) * half, half, axis=1)

    own = list(pack_weights(gate_up, down))
    got = [lax.ppermute(chunk, "member", ring) for chunk in own[:STAGGER]]
    tok_theirs = theirs(after(tokens, *own))
    tok_near = lax.ppermute(tok_theirs, "fsdp", over_x)
    up_theirs = theirs(after(grad_out, tok_theirs))
    up_near = lax.ppermute(up_theirs, "fsdp", over_x)

    def rows_from(low, high):
        pieces = []
        for c in range(low // w_rows, (high - 1) // w_rows + 1):
            first, stop = max(low, c * w_rows), min(high, (c + 1) * w_rows)
            pieces.append((c, first - c * w_rows, stop - first, first - low))
        return pieces

    def take(low, high):
        pieces = rows_from(low, high)
        kept = [(own[piece[0]],) + piece[1:] for piece in pieces]
        return assemble(winner, kept, held[:], pieces, (high - low, cols))

    rows_d = down.size // cols
    held = []
    gap = [up_theirs]
    last = STAGGER * (members - 2)
    for step in range(STAGGER, CHUNKS + last + STAGGER):
        back = got[step - STAGGER]
        if step == SEND_AT:
            d_got = lax.ppermute(after(d_mate, back), "fsdp", over_core)
            g_got = lax.ppermute(after(g_mate, back), "fsdp", over_core)
        back = after(back, *gap)
        gap = []
        if step < CHUNKS:
            back = jnp.where(is_source, own[step], back)
        held.append(back)
        gap = [back]
        if step < CHUNKS + last:
            got.append(lax.ppermute(back, "member", ring))
        if step == STAGGER:
            own += pack_moments(after(mom1_gate_up, back), mom2_gate_up, mom1_down, mom2_down)
        ready = len(held) - 1 - last
        if ready == (rows_d - 1) // w_rows:
            dn = take(0, rows_d).reshape(2, -1, rows_dn, cols)
            dn_mine = lax.dynamic_index_in_dim(dn, chip, axis=0, keepdims=False)
            dn_theirs = lax.dynamic_index_in_dim(dn, 1 - chip, axis=0, keepdims=False)
            dn_near = lax.ppermute(dn_theirs, "fsdp", over_x)
            dn_mate = lax.ppermute(dn_mine, "fsdp", over_core)
            dn_far = lax.ppermute(dn_theirs, "fsdp", over_both)
        if step == NEAR_AT:
            gap += [dn_near, dn_mate, dn_far]
        if ready == W_CHUNKS - 1:
            gu = take(rows_d, rows_all)
            gu_mate = lax.ppermute(gu, "fsdp", over_core)
        if step == GU_AT:
            pre, pre_sent = forward_gu(tokens, tok_near, after(gu, back), gu_mate)
            pre_near = lax.ppermute(pre_sent, "fsdp", over_x)
        if step == DN_AT:
            dh, dh_sent = forward_dn(
                grad_out, up_near, (after(dn_mine, back), dn_near, dn_mate, dn_far)
            )
            dh_near = lax.ppermute(dh_sent, "fsdp", over_x)
        if step == BACK_AT:
            g_own, g_mate, d_own, d_mate = backward(
                after(pre, back), pre_near, dh, dh_near, tokens, tok_near, grad_out, up_near, rows_gu, rows_dn
            )
        if step == SUM_AT:
            d_there = (
                lax.dynamic_index_in_dim(after(d_own, back), 1 - chip, axis=0, keepdims=False)
                + lax.dynamic_index_in_dim(d_got, 1 - chip, axis=0, keepdims=False)
            ).astype(jnp.bfloat16)
            d_back = lax.ppermute(d_there, "fsdp", over_x)
        if step == EARLY_AT:
            first_gu = update(
                winner,
                learning,
                0,
                EARLY,
                held[W_CHUNKS : W_CHUNKS + EARLY + last],
                (mom1_gate_up, mom2_gate_up, after(gu, back), g_own, g_got),
            )
            gap = list(first_gu)

    new_gu, new_first_gu, new_second_gu, new_dn, new_first_dn, new_second_dn = update(
        winner,
        learning,
        EARLY,
        M_CHUNKS,
        held[W_CHUNKS:],
        (mom1_gate_up, mom2_gate_up, gu, g_own, g_got),
        first_gu,
        (mom1_down, mom2_down, dn, d_own, d_got, d_back),
    )
    return (new_gu, new_dn, new_first_gu, new_second_gu, new_first_dn, new_second_dn)


def solution(mesh):
    small = mesh.shape["member"] == 4 and mesh.shape["fsdp"] == 4
    return jax.shard_map(
        on_device_four if small else on_device_any,
        mesh=mesh,
        in_specs=(
            P(("groups", "member"), "fsdp", None),
            P(("groups", "member"), "fsdp", None),
            P(("groups", "member"), "fsdp", None),
            P(("groups", "member"), "fsdp", None),
            P(("groups", "member"), "fsdp", None),
            P(("groups", "member"), "fsdp", None),
            P(("groups", "member"), "fsdp", None),
            P(("groups", "member"), "fsdp", None),
            P("groups"),
            P("groups"),
        ),
        out_specs=(
            P(("groups", "member"), "fsdp", None),
            P(("groups", "member"), "fsdp", None),
            P(("groups", "member"), "fsdp", None),
            P(("groups", "member"), "fsdp", None),
            P(("groups", "member"), "fsdp", None),
            P(("groups", "member"), "fsdp", None),
        ),
        check_vma=False,
    )
```

```python
import functools

import jax
import jax.numpy as jnp
from jax import lax
from jax.experimental import pallas as pl
from jax.experimental.pallas import tpu as pltpu
from jax.sharding import PartitionSpec as P

beta_one = 0.9
beta_two = 0.95
epsilon = 1e-08
decay = 0.1


def spread(block, axis, source):
    block = jnp.where(lax.axis_index(axis) == source, block, jnp.zeros_like(block))
    return lax.psum(block, axis)


def adamw(weight, grad, first, second, rate):
    first_new = beta_one * first + (1.0 - beta_one) * grad
    second_new = beta_two * second + (1.0 - beta_two) * grad * grad
    wide = weight.astype(jnp.float32)
    updated = wide - rate * (first_new / (jnp.sqrt(second_new) + epsilon) + decay * wide)
    return (updated.astype(jnp.bfloat16), first_new, second_new)


def on_device_any(
    tokens,
    grad_out,
    gate_up,
    down,
    mom1_gate_up,
    mom2_gate_up,
    mom1_down,
    mom2_down,
    learning,
    winner,
):
    members = lax.axis_size("member")
    member_index = lax.axis_index("member")
    rows_in = tokens[0]
    upstream = grad_out[0]
    width = rows_in.shape[1]
    units = gate_up.shape[2] // 2
    shard_gu = gate_up[0]
    shard_dn = down[0]
    cut = shard_gu.size // members

    def joined(first_part, second_part):
        return jnp.concatenate(
            [first_part.reshape(members, -1), second_part.reshape(members, -1)], axis=1
        )

    def parted(flat):
        return (flat[:, :cut].reshape(shard_gu.shape), flat[:, cut:].reshape(shard_dn.shape))

    own_source = winner[member_index]

    def take_root(root, carry):
        sent_gu, sent_dn = (spread(shard_gu, "member", root), spread(shard_dn, "member", root))
        wanted = own_source == root
        return (jnp.where(wanted, sent_gu, carry[0]), jnp.where(wanted, sent_dn, carry[1]))

    copied_gu, copied_dn = lax.fori_loop(0, members, take_root, (shard_gu, shard_dn))
    first_gu, first_dn = parted(
        lax.all_to_all(
            jnp.take(
                lax.all_to_all(
                    joined(mom1_gate_up[0], mom1_down[0]).astype(jnp.bfloat16),
                    "member",
                    split_axis=0,
                    concat_axis=0,
                    tiled=True,
                ).astype(jnp.float32),
                winner,
                axis=0,
            ).astype(jnp.bfloat16),
            "member",
            split_axis=0,
            concat_axis=0,
            tiled=True,
        ).astype(jnp.float32)
    )
    second_gu, second_dn = parted(
        lax.all_to_all(
            jnp.take(
                lax.all_to_all(
                    joined(mom2_gate_up[0], mom2_down[0]).astype(jnp.bfloat16),
                    "member",
                    split_axis=0,
                    concat_axis=0,
                    tiled=True,
                ).astype(jnp.float32),
                winner,
                axis=0,
            ).astype(jnp.bfloat16),
            "member",
            split_axis=0,
            concat_axis=0,
            tiled=True,
        ).astype(jnp.float32)
    )
    rate = learning[winner[member_index]]
    columns = rows_in
    preact = jnp.dot(
        columns,
        lax.all_gather(copied_gu, "fsdp", axis=0, tiled=True),
        preferred_element_type=jnp.float32,
    ) * width ** (-0.5)
    gate = preact[:, :units]
    upper = preact[:, units:]
    sigma = jax.nn.sigmoid(gate)
    active = gate * sigma
    hidden = (active * upper).astype(jnp.bfloat16)
    dhidden = lax.dot_general(
        upstream,
        lax.all_gather(copied_dn, "fsdp", axis=0, tiled=True),
        (((1,), (1,)), ((), ())),
        preferred_element_type=jnp.float32,
    ) * units ** (-0.5)
    dgate = dhidden * upper * (sigma * (1.0 + gate * (1.0 - sigma)))
    dupper = dhidden * active
    dpreact = (jnp.concatenate([dgate, dupper], axis=1) * width ** (-0.5)).astype(jnp.bfloat16)
    columns = rows_in
    grad_gu = lax.psum_scatter(
        lax.dot_general(
            columns, dpreact, (((0,), (0,)), ((), ())), preferred_element_type=jnp.float32
        ).astype(jnp.bfloat16),
        "fsdp",
        scatter_dimension=0,
        tiled=True,
    ).astype(jnp.float32)
    columns = hidden
    product = lax.dot_general(
        columns, upstream, (((0,), (0,)), ((), ())), preferred_element_type=jnp.float32
    )
    grad_dn = lax.psum_scatter(
        (product * units ** (-0.5)).astype(jnp.bfloat16), "fsdp", scatter_dimension=0, tiled=True
    ).astype(jnp.float32)
    new_gu, new_first_gu, new_second_gu = adamw(copied_gu, grad_gu, first_gu, second_gu, rate)
    new_dn, new_first_dn, new_second_dn = adamw(copied_dn, grad_dn, first_dn, second_dn, rate)
    return (
        new_gu[None],
        new_dn[None],
        new_first_gu[None],
        new_second_gu[None],
        new_first_dn[None],
        new_second_dn[None],
    )


ANY = pl.BlockSpec(memory_space=pl.ANY)
SMEM = pl.BlockSpec(memory_space=pltpu.SMEM)
VMEM = pl.BlockSpec(memory_space=pltpu.VMEM)
STAGGER = 2
W_CHUNKS = 4
M_CHUNKS = 8
CHUNKS = W_CHUNKS + M_CHUNKS
EARLY = 6
NEAR_AT = 8
SEND_AT = 14
GU_AT = 10
DN_AT = 11
BACK_AT = 13
SUM_AT = 15
EARLY_AT = 16


def grant(mib):
    return pltpu.CompilerParams(vmem_limit_bytes=mib * 1024 * 1024)


def cost(flops, moved):
    return pl.CostEstimate(flops=flops, bytes_accessed=moved, transcendentals=0)


def in_hbm(*arrays):
    return [pltpu.with_memory_space_constraint(array, pltpu.HBM) for array in arrays]


def in_vmem(*arrays):
    return [pltpu.with_memory_space_constraint(array, pltpu.VMEM) for array in arrays]


def after(value, *others):
    return lax.optimization_barrier((value,) + others)[0]


def mode_of(winner_ref, members):
    member = lax.axis_index("member")
    source = 0
    for other in range(members):
        source = jnp.where(winner_ref[other] != other, winner_ref[other], source)
    return jnp.where(
        winner_ref[member] == member, 0, lax.rem(member - source + members, members)
    )


def chip_and_core():
    index = lax.axis_index("fsdp")
    return index // 2, lax.rem(index, 2)


def start_all(pairs, sems):
    copies = [pltpu.make_async_copy(a, b, sems.at[n]) for n, (a, b) in enumerate(pairs)]
    for copy in copies:
        copy.start()
    return copies


def wait_all(copies):
    for copy in copies:
        copy.wait()


def assemble(winner, own, held, pieces, out_shape):
    members = winner.shape[0]
    arrays = [array for array, _, _, _ in own]

    def kernel(winner_ref, *refs):
        own_refs, came = refs[: len(own)], refs[len(own) : len(own) + len(held)]
        out, sems = refs[len(own) + len(held) :]
        mode = mode_of(winner_ref, members)

        def move(refs, places):
            wait_all(
                start_all(
                    [
                        (ref.at[pl.ds(start, rows)], out.at[pl.ds(to, rows)])
                        for ref, (_, start, rows, to) in zip(refs, places)
                    ],
                    sems,
                )
            )

        @pl.when(mode == 0)
        def _():
            move(own_refs, own)

        for hop in range(members - 1):

            @pl.when(mode == hop + 1)
            def _():
                move([came[place + STAGGER * hop] for place, _, _, _ in pieces], pieces)

    return pl.pallas_call(
        kernel,
        out_shape=jax.ShapeDtypeStruct(out_shape, jnp.bfloat16),
        in_specs=[SMEM] + [ANY] * (len(own) + len(held)),
        out_specs=VMEM,
        scratch_shapes=[pltpu.SemaphoreType.DMA((max(len(own), len(pieces)),))],
        compiler_params=grant(4),
        cost_estimate=cost(0, 4 * out_shape[0] * out_shape[1]),
        name="assemble",
    )(winner, *arrays, *held)


def pack_moments(m1_gu, m2_gu, m1_dn, m2_dn):
    _, rows_gu, cols = m1_gu.shape
    _, rows_dn, width = m1_dn.shape
    part = rows_gu // M_CHUNKS
    wide = width // M_CHUNKS
    blocks = wide // cols
    each = part + blocks * rows_dn

    def kernel(m1g, m2g, m1d, m2d, *refs):
        outs, (gu, dn, sems) = refs[:M_CHUNKS], refs[M_CHUNKS:]
        copies = []
        for n in range(M_CHUNKS):
            rows, columns = pl.ds(n * part, part), pl.ds(n * wide, wide)
            copies.append(
                start_all(
                    [
                        (m1g.at[0, rows], gu.at[0, rows]),
                        (m2g.at[0, rows], gu.at[1, rows]),
                        (m1d.at[0, :, columns], dn.at[0, :, columns]),
                        (m2d.at[0, :, columns], dn.at[1, :, columns]),
                    ],
                    sems.at[n],
                )
            )
        for n, out in enumerate(outs):
            wait_all(copies[n])
            for k in range(2):
                base = k * each
                out[base : base + part] = gu[k, n * part : (n + 1) * part].astype(out.dtype)
                for b in range(blocks):
                    at = (n * blocks + b) * cols
                    to = base + part + b * rows_dn
                    out[to : to + rows_dn] = dn[k, :, at : at + cols].astype(out.dtype)

    return pl.pallas_call(
        kernel,
        out_shape=tuple(
            jax.ShapeDtypeStruct((2 * each, cols), jnp.bfloat16) for _ in range(M_CHUNKS)
        ),
        in_specs=[ANY] * 4,
        out_specs=(VMEM,) * M_CHUNKS,
        scratch_shapes=[
            pltpu.VMEM((2, rows_gu, cols), jnp.float32),
            pltpu.VMEM((2, rows_dn, width), jnp.float32),
            pltpu.SemaphoreType.DMA((M_CHUNKS, 4)),
        ],
        compiler_params=grant(8),
        cost_estimate=cost(0, 12 * (m1_gu.size + m1_dn.size)),
        name="pack_moments",
    )(*in_hbm(m1_gu, m2_gu, m1_dn, m2_dn))


def pack_weights(gate_up, down):
    _, rows_gu, cols = gate_up.shape
    _, rows_dn, width = down.shape
    blocks = width // cols
    total = rows_gu + blocks * rows_dn
    size = total // W_CHUNKS

    def kernel(gu_ref, down_ref, *refs):
        outs, (buf, sems) = refs[:W_CHUNKS], refs[W_CHUNKS:]
        pairs = [(down_ref.at[0], buf)]
        for n, out in enumerate(outs):
            low = max(n * size, blocks * rows_dn)
            rows = (n + 1) * size - low
            if rows > 0:
                source = gu_ref.at[0, pl.ds(low - blocks * rows_dn, rows)]
                pairs.append((source, out.at[pl.ds(low - n * size, rows)]))
        copies = start_all(pairs, sems)
        copies[0].wait()
        for b in range(blocks):
            n, to = divmod(b * rows_dn, size)
            outs[n][to : to + rows_dn] = buf[:, b * cols : (b + 1) * cols]
        wait_all(copies[1:])

    return pl.pallas_call(
        kernel,
        out_shape=tuple(jax.ShapeDtypeStruct((size, cols), down.dtype) for _ in range(W_CHUNKS)),
        in_specs=[ANY, ANY],
        out_specs=(VMEM,) * W_CHUNKS,
        scratch_shapes=[
            pltpu.VMEM((rows_dn, width), down.dtype),
            pltpu.SemaphoreType.DMA((W_CHUNKS + 1,)),
        ],
        compiler_params=grant(4),
        cost_estimate=cost(0, 4 * total * cols),
        name="pack_weights",
    )(*in_hbm(gate_up, down))


def partial(count, columns):
    return (
        jax.ShapeDtypeStruct((2 * count, columns), jnp.float32),
        jax.ShapeDtypeStruct((2 * count, columns), jnp.bfloat16),
    )


def forward_gu(tokens, tok_near, gu, gu_mate):
    _, count, width = tokens.shape
    half = width // 2
    rows, cols = gu.shape

    def kernel(tok_r, tokn_r, gu_r, gum_r, out, sent, tok, gub, sems):
        chip, core = chip_and_core()
        mine = pl.ds(pl.multiple_of(chip * half, half), half)
        first = pl.ds(pl.multiple_of(core * rows, rows), rows)
        second = pl.ds(pl.multiple_of((1 - core) * rows, rows), rows)
        pairs = [
            (gu_r, gub.at[first]),
            (gum_r, gub.at[second]),
            (tok_r.at[0, :, mine], tok.at[pl.ds(0, count)]),
            (tokn_r, tok.at[pl.ds(count, count)]),
        ]
        wait_all(start_all(pairs, sems))
        pre = jnp.dot(tok[...], gub[...], preferred_element_type=jnp.float32)
        out[...] = pre
        sent[...] = pre.astype(sent.dtype)

    return pl.pallas_call(
        kernel,
        out_shape=partial(count, cols),
        in_specs=[ANY] * 4,
        out_specs=(VMEM, VMEM),
        scratch_shapes=[
            pltpu.VMEM((2 * count, half), jnp.bfloat16),
            pltpu.VMEM((half, cols), jnp.bfloat16),
            pltpu.SemaphoreType.DMA((4,)),
        ],
        compiler_params=grant(8),
        cost_estimate=cost(4 * count * half * cols, 3 * 1024 * 1024),
        name="forward_gu",
    )(*in_hbm(tokens), tok_near, *in_vmem(gu, gu_mate))


def forward_dn(grad_out, up_near, parts):
    _, count, width = grad_out.shape
    half = width // 2
    blocks, rows, cols = parts[0].shape
    units = 4 * rows

    def kernel(up_r, upn_r, mine_r, near_r, mate_r, far_r, out, sent, up, dnb, sems):
        chip, core = chip_and_core()
        mine = pl.ds(pl.multiple_of(chip * half, half), half)
        pairs = [
            (up_r.at[0, :, mine], up.at[pl.ds(0, count)]),
            (upn_r, up.at[pl.ds(count, count)]),
            (mine_r, dnb.at[:, chip, core]),
            (near_r, dnb.at[:, 1 - chip, core]),
            (mate_r, dnb.at[:, chip, 1 - core]),
            (far_r, dnb.at[:, 1 - chip, 1 - core]),
        ]
        wait_all(start_all(pairs, sems))
        dh = jnp.zeros((2 * count, units), jnp.float32)
        for b in range(blocks):
            dh += lax.dot_general(
                up[:, b * cols : (b + 1) * cols],
                dnb[b].reshape(units, cols),
                (((1,), (1,)), ((), ())),
                preferred_element_type=jnp.float32,
            )
        out[...] = dh
        sent[...] = dh.astype(sent.dtype)

    return pl.pallas_call(
        kernel,
        out_shape=partial(count, units),
        in_specs=[ANY] * 6,
        out_specs=(VMEM, VMEM),
        scratch_shapes=[
            pltpu.VMEM((2 * count, half), jnp.bfloat16),
            pltpu.VMEM((blocks, 2, 2, rows, cols), jnp.bfloat16),
            pltpu.SemaphoreType.DMA((6,)),
        ],
        compiler_params=grant(8),
        cost_estimate=cost(4 * count * half * units, 3 * 1024 * 1024),
        name="forward_dn",
    )(*in_hbm(grad_out), up_near, *in_vmem(*parts))


def backward(pre, pre_near, dh, dh_near, tokens, tok_near, grad_out, up_near, rows, rows_dn):
    _, count, width = tokens.shape
    half = width // 2
    units = 4 * rows_dn
    cols = 2 * units
    blocks = half // cols

    def kernel(pre_r, pren_r, dh_r, dhn_r, tok_r, tokn_r, up_r, upn_r, g_own, g_mate, d_own, d_mate, tok, tokm, up, res, sems):
        chip, core = chip_and_core()
        mine = pl.ds(pl.multiple_of(chip * half, half), half)
        first = pl.multiple_of(core * rows, rows)
        second = pl.multiple_of((1 - core) * rows, rows)
        here = pl.multiple_of(chip * half, half)
        pairs = [
            (up_r.at[0, :, mine], up.at[pl.ds(0, count)]),
            (upn_r, up.at[pl.ds(count, count)]),
            (tok_r.at[0, :, pl.ds(here + second, rows)], tokm.at[pl.ds(0, count)]),
            (tokn_r.at[:, pl.ds(second, rows)], tokm.at[pl.ds(count, count)]),
            (tok_r.at[0, :, pl.ds(here + first, rows)], tok.at[pl.ds(0, count)]),
            (tokn_r.at[:, pl.ds(first, rows)], tok.at[pl.ds(count, count)]),
        ]
        copies = start_all(pairs, sems)

        def whole(own, near):
            return own[...] + jnp.concatenate([near[count:], near[:count]]).astype(jnp.float32)

        full = whole(pre_r, pren_r) * width ** (-0.5)
        gate = full[:, :units]
        upper = full[:, units:]
        dhidden = whole(dh_r, dhn_r) * units ** (-0.5)
        sigma = jax.nn.sigmoid(gate)
        active = gate * sigma
        hidden = (active * upper).astype(jnp.bfloat16)
        dgate = dhidden * upper * (sigma * (1.0 + gate * (1.0 - sigma)))
        dupper = dhidden * active
        dpre = (jnp.concatenate([dgate, dupper], axis=1) * width ** (-0.5)).astype(jnp.bfloat16)
        over_tokens = (((0,), (0,)), ((), ()))
        wait_all(copies[:2])
        for b in range(blocks):
            res[b] = lax.dot_general(
                hidden, up[:, b * cols : (b + 1) * cols], over_tokens, preferred_element_type=jnp.float32
            ) * units ** (-0.5)
        for b in range(blocks):
            for x in range(2):
                base = x * 2 * rows_dn
                d_own[x, b] = res[b, pl.ds(pl.multiple_of(base + core * rows_dn, rows_dn), rows_dn)]
                d_mate[x, b] = res[
                    b, pl.ds(pl.multiple_of(base + (1 - core) * rows_dn, rows_dn), rows_dn)
                ].astype(d_mate.dtype)
        wait_all(copies[2:4])
        g_mate[...] = lax.dot_general(
            tokm[...], dpre, over_tokens, preferred_element_type=jnp.float32
        ).astype(g_mate.dtype)
        wait_all(copies[4:])
        g_own[...] = lax.dot_general(tok[...], dpre, over_tokens, preferred_element_type=jnp.float32)

    f32, bf16 = jnp.float32, jnp.bfloat16
    dn_shape = (2, blocks, rows_dn, cols)
    return pl.pallas_call(
        kernel,
        out_shape=(
            pltpu.VMEM((rows, cols), f32),
            pltpu.VMEM((rows, cols), bf16),
            pltpu.VMEM(dn_shape, f32),
            pltpu.VMEM(dn_shape, bf16),
        ),
        in_specs=[VMEM] * 4 + [ANY] * 4,
        out_specs=(VMEM,) * 4,
        scratch_shapes=[
            pltpu.VMEM((2 * count, rows), bf16),
            pltpu.VMEM((2 * count, rows), bf16),
            pltpu.VMEM((2 * count, half), bf16),
            pltpu.VMEM((blocks, units, cols), f32),
            pltpu.SemaphoreType.DMA((6,)),
        ],
        compiler_params=grant(16),
        cost_estimate=cost(4 * count * half * (cols + units), 6 * 1024 * 1024),
        name="backward",
    )(pre, pre_near, dh, dh_near, *in_hbm(tokens), tok_near, *in_hbm(grad_out), up_near)


def adamw_part(weight, grad, first, second, rate):
    first_new = beta_one * first + (1.0 - beta_one) * grad
    second_new = beta_two * second + (1.0 - beta_two) * grad * grad
    wide = weight.astype(jnp.float32)
    updated = wide - rate * (first_new / (jnp.sqrt(second_new) + epsilon) + decay * wide)
    return updated.astype(jnp.bfloat16), first_new, second_new


def start_moments(mode, members, own_pairs, came_pairs, sems):
    @pl.when(mode == 0)
    def _():
        for n, pairs in enumerate(own_pairs):
            for k, (a, b) in enumerate(pairs):
                pltpu.make_async_copy(a, b, sems.at[n, k]).start()

    for hop in range(members - 1):

        @pl.when(mode == hop + 1)
        def _():
            for n, pairs in enumerate(came_pairs[hop]):
                for k, (a, b) in enumerate(pairs):
                    pltpu.make_async_copy(a, b, sems.at[n, k]).start()


def wait_moments(mode, n, own_pairs, came_pairs, sems):
    @pl.when(mode == 0)
    def _():
        for k, (a, b) in enumerate(own_pairs[n]):
            pltpu.make_async_copy(a, b, sems.at[n, k]).wait()

    @pl.when(mode != 0)
    def _():
        for k, (a, b) in enumerate(came_pairs[0][n]):
            pltpu.make_async_copy(a, b, sems.at[n, k]).wait()


def gate_up_rows(mode, rate, members, low, high, each, ins, came, outs, scratch):
    m1_r, m2_r, gu_r, go_r, gm_r = ins
    n_w, n_1, n_2 = outs
    bgu, bgo, bgm, own, moved, o_w, o_1, o_2, sems, msems, osems = scratch
    part = m1_r.shape[1] // M_CHUNKS
    start, count = low * part, high - low
    span = pl.ds(start, count * part)
    own_pairs = [
        [
            (m1_r.at[0, pl.ds(start + n * part, part)], own.at[0, pl.ds(n * part, part)]),
            (m2_r.at[0, pl.ds(start + n * part, part)], own.at[1, pl.ds(n * part, part)]),
        ]
        for n in range(count)
    ]
    came_pairs = [
        [
            [
                (came[low + n + STAGGER * hop].at[pl.ds(0, part)], moved.at[n, 0]),
                (came[low + n + STAGGER * hop].at[pl.ds(each, part)], moved.at[n, 1]),
            ]
            for n in range(count)
        ]
        for hop in range(members - 1)
    ]
    copies = start_all([(gu_r.at[span], bgu), (go_r.at[span], bgo), (gm_r.at[span], bgm)], sems)
    start_moments(mode, members, own_pairs, came_pairs, msems)

    def finish():
        wait_all(copies)
        sent = []
        for n in range(count):
            wait_moments(mode, n, own_pairs, came_pairs, msems)
            at = slice(n * part, (n + 1) * part)
            first = jnp.where(mode == 0, own[0, at], moved[n, 0].astype(jnp.float32))
            second = jnp.where(mode == 0, own[1, at], moved[n, 1].astype(jnp.float32))
            grad = bgo[at] + bgm[at].astype(jnp.float32)
            o_w[at], o_1[at], o_2[at] = adamw_part(bgu[at], grad, first, second, rate)
            here, there = pl.ds(n * part, part), pl.ds(start + n * part, part)
            sent += start_all(
                [
                    (o_w.at[here], n_w.at[0, there]),
                    (o_1.at[here], n_1.at[0, there]),
                    (o_2.at[here], n_2.at[0, there]),
                ],
                osems.at[n],
            )
        return sent

    return finish


def down_rows(mode, rate, members, each, ins, came, outs, scratch):
    m1_r, m2_r, dn_r, do_r, dm_r, gb_r = ins
    n_w, n_1, n_2 = outs
    bdn, bdo, bdm, bgb, grad, own, moved, o_w, o_1, o_2, sems, msems, osems = scratch
    _, rows, width = m1_r.shape
    _, blocks, _, cols = dn_r.shape
    per = 2 * blocks // M_CHUNKS
    size = per * rows
    base = each - size
    chip, _ = chip_and_core()
    spans = [pl.ds(n * per * cols, per * cols) for n in range(M_CHUNKS)]
    own_pairs = [
        [(m1_r.at[0, :, span], own.at[0, :, span]), (m2_r.at[0, :, span], own.at[1, :, span])]
        for span in spans
    ]
    came_pairs = [
        [
            [
                (came[n + STAGGER * hop].at[pl.ds(base, size)], moved.at[n, 0]),
                (came[n + STAGGER * hop].at[pl.ds(each + base, size)], moved.at[n, 1]),
            ]
            for n in range(M_CHUNKS)
        ]
        for hop in range(members - 1)
    ]
    copies = start_all([(dn_r, bdn), (do_r.at[chip], bdo), (dm_r.at[chip], bdm), (gb_r, bgb)], sems)
    start_moments(mode, members, own_pairs, came_pairs, msems)

    def finish():
        wait_all(copies)
        grad[chip] = bdo[...] + bdm[...].astype(jnp.float32)
        grad[1 - chip] = bgb[...].astype(jnp.float32)
        sent = []
        for n in range(M_CHUNKS):
            wait_moments(mode, n, own_pairs, came_pairs, msems)
            for i in range(per):
                at = slice((n * per + i) * cols, (n * per + i + 1) * cols)
                sub = slice(i * rows, (i + 1) * rows)
                first = jnp.where(mode == 0, own[0, :, at], moved[n, 0, sub].astype(jnp.float32))
                second = jnp.where(mode == 0, own[1, :, at], moved[n, 1, sub].astype(jnp.float32))
                side, b = divmod(n * per + i, blocks)
                o_w[:, at], o_1[:, at], o_2[:, at] = adamw_part(
                    bdn[side, b], grad[side, b], first, second, rate
                )
            if n % 2 == 1:
                at = pl.ds((n - 1) * per * cols, 2 * per * cols)
                sent += start_all(
                    [
                        (o_w.at[:, at], n_w.at[0, :, at]),
                        (o_1.at[:, at], n_1.at[0, :, at]),
                        (o_2.at[:, at], n_2.at[0, :, at]),
                    ],
                    osems.at[n // 2],
                )
        return sent

    return finish


def update(winner, learning, low, high, held, gate_up_side, done=(), down_side=()):
    members = winner.shape[0]
    m1, m2, gu, g_own, g_got = gate_up_side
    _, rows, cols = m1.shape
    part = rows // M_CHUNKS
    each = held[0].shape[0] // 2
    count = high - low
    size = count * part
    f32, bf16 = jnp.float32, jnp.bfloat16
    scratch = [
        pltpu.VMEM((size, cols), bf16),
        pltpu.VMEM((size, cols), f32),
        pltpu.VMEM((size, cols), bf16),
        pltpu.VMEM((2, size, cols), f32),
        pltpu.VMEM((count, 2, part, cols), bf16),
        pltpu.VMEM((size, cols), bf16),
        pltpu.VMEM((size, cols), f32),
        pltpu.VMEM((size, cols), f32),
        pltpu.SemaphoreType.DMA((3,)),
        pltpu.SemaphoreType.DMA((count, 2)),
        pltpu.SemaphoreType.DMA((count, 3)),
    ]
    shapes = [jax.ShapeDtypeStruct((1, rows, cols), t) for t in (bf16, f32, f32)]
    operands = [*in_hbm(m1, m2), *in_vmem(gu, g_own, g_got)]
    if down_side:
        n1, n2, dn, d_own, d_got, d_back = down_side
        _, rows_dn, width = n1.shape
        half = dn.shape[1:]
        moved = (width // cols // M_CHUNKS) * rows_dn
        scratch += [
            pltpu.VMEM((2,) + half, bf16),
            pltpu.VMEM(half, f32),
            pltpu.VMEM(half, bf16),
            pltpu.VMEM(half, bf16),
            pltpu.VMEM((2,) + half, f32),
            pltpu.VMEM((2, rows_dn, width), f32),
            pltpu.VMEM((M_CHUNKS, 2, moved, cols), bf16),
            pltpu.VMEM((rows_dn, width), bf16),
            pltpu.VMEM((rows_dn, width), f32),
            pltpu.VMEM((rows_dn, width), f32),
            pltpu.SemaphoreType.DMA((4,)),
            pltpu.SemaphoreType.DMA((M_CHUNKS, 2)),
            pltpu.SemaphoreType.DMA((M_CHUNKS // 2, 3)),
        ]
        shapes += [jax.ShapeDtypeStruct((1, rows_dn, width), t) for t in (bf16, f32, f32)]
        operands += [*in_hbm(n1, n2), *in_vmem(dn, d_own, d_got, d_back)]
    fixed = len(operands)

    def kernel(winner_ref, rate_ref, *refs):
        ins, refs = refs[:fixed], refs[fixed:]
        came, refs = refs[: len(held)], refs[len(held) + len(done) :]
        outs, temps = refs[: len(shapes)], refs[len(shapes) :]
        mode = mode_of(winner_ref, members)
        rate = rate_ref[winner_ref[lax.axis_index("member")]]
        finish = [
            gate_up_rows(mode, rate, members, low, high, each, ins[:5], came, outs[:3], temps[:11])
        ]
        if down_side:
            finish.append(down_rows(mode, rate, members, each, ins[5:], came, outs[3:], temps[11:]))
        sent = [copy for part in finish for copy in part()]
        wait_all(sent)

    return pl.pallas_call(
        kernel,
        out_shape=tuple(shapes),
        in_specs=[SMEM, SMEM] + [ANY] * (fixed + len(held) + len(done)),
        out_specs=(ANY,) * len(shapes),
        scratch_shapes=scratch,
        input_output_aliases={2 + fixed + len(held) + n: n for n in range(len(done))},
        compiler_params=grant(16),
        cost_estimate=cost(0, 22 * size * cols),
        name="update",
    )(winner, learning, *operands, *in_vmem(*held), *done)


def on_device_four(
    tokens,
    grad_out,
    gate_up,
    down,
    mom1_gate_up,
    mom2_gate_up,
    mom1_down,
    mom2_down,
    learning,
    winner,
):
    members = lax.axis_size("member")
    member_index = lax.axis_index("member")
    fsdp_index = lax.axis_index("fsdp")
    chip = fsdp_index // 2
    over_x = [(0, 2), (2, 0), (1, 3), (3, 1)]
    over_core = [(0, 1), (1, 0), (2, 3), (3, 2)]
    over_both = [(0, 3), (3, 0), (1, 2), (2, 1)]
    ring = [(i, (i + 1) % members) for i in range(members)]
    half = tokens.shape[2] // 2
    _, rows_gu, cols = gate_up.shape
    rows_dn = down.shape[1]
    rows_all = rows_gu + down.size // cols
    w_rows = rows_all // W_CHUNKS

    indices = jnp.arange(members, dtype=winner.dtype)
    is_source = jnp.any((winner == member_index) & (indices != member_index))

    def theirs(x):
        return lax.dynamic_slice_in_dim(x[0], (1 - chip) * half, half, axis=1)

    own = list(pack_weights(gate_up, down))
    got = [lax.ppermute(chunk, "member", ring) for chunk in own[:STAGGER]]
    tok_theirs = theirs(after(tokens, *own))
    tok_near = lax.ppermute(tok_theirs, "fsdp", over_x)
    up_theirs = theirs(after(grad_out, tok_theirs))
    up_near = lax.ppermute(up_theirs, "fsdp", over_x)

    def rows_from(low, high):
        pieces = []
        for c in range(low // w_rows, (high - 1) // w_rows + 1):
            first, stop = max(low, c * w_rows), min(high, (c + 1) * w_rows)
            pieces.append((c, first - c * w_rows, stop - first, first - low))
        return pieces

    def take(low, high):
        pieces = rows_from(low, high)
        kept = [(own[piece[0]],) + piece[1:] for piece in pieces]
        return assemble(winner, kept, held[:], pieces, (high - low, cols))

    rows_d = down.size // cols
    held = []
    gap = []
    last = STAGGER * (members - 2)
    for step in range(STAGGER, CHUNKS + last + STAGGER):
        back = got[step - STAGGER]
        if step == SEND_AT:
            d_got = lax.ppermute(after(d_mate, back), "fsdp", over_core)
            g_got = lax.ppermute(after(g_mate, back), "fsdp", over_core)
        back = after(back, *gap)
        gap = []
        if step < CHUNKS:
            back = jnp.where(is_source, own[step], back)
        held.append(back)
        gap = [back]
        if step < CHUNKS + last:
            got.append(lax.ppermute(back, "member", ring))
        if step == STAGGER:
            own += pack_moments(after(mom1_gate_up, back), mom2_gate_up, mom1_down, mom2_down)
        ready = len(held) - 1 - last
        if ready == (rows_d - 1) // w_rows:
            dn = take(0, rows_d).reshape(2, -1, rows_dn, cols)
            dn_mine = lax.dynamic_index_in_dim(dn, chip, axis=0, keepdims=False)
            dn_theirs = lax.dynamic_index_in_dim(dn, 1 - chip, axis=0, keepdims=False)
            dn_near = lax.ppermute(dn_theirs, "fsdp", over_x)
            dn_mate = lax.ppermute(dn_mine, "fsdp", over_core)
            dn_far = lax.ppermute(dn_theirs, "fsdp", over_both)
        if step == NEAR_AT:
            gap += [dn_near, dn_mate, dn_far]
        if ready == W_CHUNKS - 1:
            gu = take(rows_d, rows_all)
            gu_mate = lax.ppermute(gu, "fsdp", over_core)
        if step == GU_AT:
            pre, pre_sent = forward_gu(tokens, tok_near, after(gu, back), gu_mate)
            pre_near = lax.ppermute(pre_sent, "fsdp", over_x)
        if step == DN_AT:
            dh, dh_sent = forward_dn(
                grad_out, up_near, (after(dn_mine, back), dn_near, dn_mate, dn_far)
            )
            dh_near = lax.ppermute(dh_sent, "fsdp", over_x)
        if step == BACK_AT:
            g_own, g_mate, d_own, d_mate = backward(
                after(pre, back), pre_near, dh, dh_near, tokens, tok_near, grad_out, up_near, rows_gu, rows_dn
            )
        if step == SUM_AT:
            d_there = (
                lax.dynamic_index_in_dim(after(d_own, back), 1 - chip, axis=0, keepdims=False)
                + lax.dynamic_index_in_dim(d_got, 1 - chip, axis=0, keepdims=False)
            ).astype(jnp.bfloat16)
            d_back = lax.ppermute(d_there, "fsdp", over_x)
        if step == EARLY_AT:
            first_gu = update(
                winner,
                learning,
                0,
                EARLY,
                held[W_CHUNKS : W_CHUNKS + EARLY + last],
                (mom1_gate_up, mom2_gate_up, after(gu, back), g_own, g_got),
            )
            gap = list(first_gu)

    new_gu, new_first_gu, new_second_gu, new_dn, new_first_dn, new_second_dn = update(
        winner,
        learning,
        EARLY,
        M_CHUNKS,
        held[W_CHUNKS:],
        (mom1_gate_up, mom2_gate_up, gu, g_own, g_got),
        first_gu,
        (mom1_down, mom2_down, dn, d_own, d_got, d_back),
    )
    return (new_gu, new_dn, new_first_gu, new_second_gu, new_first_dn, new_second_dn)


def solution(mesh):
    small = mesh.shape["member"] == 4 and mesh.shape["fsdp"] == 4
    return jax.shard_map(
        on_device_four if small else on_device_any,
        mesh=mesh,
        in_specs=(
            P(("groups", "member"), "fsdp", None),
            P(("groups", "member"), "fsdp", None),
            P(("groups", "member"), "fsdp", None),
            P(("groups", "member"), "fsdp", None),
            P(("groups", "member"), "fsdp", None),
            P(("groups", "member"), "fsdp", None),
            P(("groups", "member"), "fsdp", None),
            P(("groups", "member"), "fsdp", None),
            P("groups"),
            P("groups"),
        ),
        out_specs=(
            P(("groups", "member"), "fsdp", None),
            P(("groups", "member"), "fsdp", None),
            P(("groups", "member"), "fsdp", None),
            P(("groups", "member"), "fsdp", None),
            P(("groups", "member"), "fsdp", None),
            P(("groups", "member"), "fsdp", None),
        ),
        check_vma=False,
    )
```
